256 devices in a mesh: dp: 8 (over x, core), tm: 8 (over z_hi, y), height: 4 (over z_lo).
Axes of the slice: x: 4, y: 4, z: 8 (z_hi: 2, z_lo: 4; z = z_hi * 4 + z_lo), core: 2. Of those that a mesh axis runs over, the one named last changes fastest.
Arguments:
- queries: bfloat16 [8, 4, 384, 3072], P('tm', 'height', None, 'dp'), may hold values from -6 to 6
- key_vectors: bfloat16 [8, 4, 384, 3072], P('tm', 'height', None, 'dp'), may hold values from -6 to 6
- value_vectors: bfloat16 [8, 4, 384, 3072], P('tm', 'height', None, 'dp'), may hold values from -6 to 6
- out_grads: bfloat16 [8, 4, 384, 3072], P('tm', 'height', None, 'dp'), may hold values from -9 to 9
- query_gain: float32 [128], replicated, may hold values from 0.6 to 5.5
- key_gain: float32 [128], replicated, may hold values from 0.6 to 5.5
- frame_counts: int32 [8], replicated, may hold values from 1 to 6, as said below
- row_counts: int32 [4], replicated, may hold values from 1 to 8, as said below
Outputs:
- d_queries: bfloat16 [8, 4, 384, 3072], P('tm', 'height', None, 'dp')
- d_keys: bfloat16 [8, 4, 384, 3072], P('tm', 'height', None, 'dp')
- d_values: bfloat16 [8, 4, 384, 3072], P('tm', 'height', None, 'dp')
- gain_grads: float32 [2, 128], replicated
The draws below stay inside these ranges and needn't reach their ends.
Inputs may be any that keep to these rules, and one draw needn't show every extreme that they name: `frame_counts`: exactly one time tile has all 6 frames; the others have fewer. `row_counts`: exactly one height tile has all 8 rows; the others have fewer.
All inputs are finite; a program needn't handle non-finite values.
Results may differ from the reference program's by a relative error of at most 0.004.
The reference program's roundings to bfloat16 on the way count: a program that leaves them out, or rounds other values in their place, can miss the bound.
Values may be sent and summed in bfloat16 or wider, within the bound.
No kernel may reach another device: no remote copies, remote signals or barrier semaphores. Data moves between devices by JAX's collectives and lax.ppermute only.
A program may use at most 64 MiB of HBM per device.

```python
import math
import jax
import jax.numpy as jnp
from jax import lax

HD = 128
FEATURES = 3072
TF = 6
TH = 8
TW = 8
ROWS = 384
NTT = 8
NHT = 4


def padded_counts(key, count, limit):
    full_key, rest_key = jax.random.split(key, 2)
    full_at = jax.random.randint(full_key, (), 0, count)
    rest = jax.random.randint(rest_key, (count,), 1, limit)
    return jnp.where(jnp.arange(count, dtype=jnp.int32) == full_at, limit, rest).astype(jnp.int32)


def draw_queries(key, part):
    key = jax.random.fold_in(key, 11)
    sample = jnp.clip(jax.random.normal(key, (NTT, NHT, ROWS, FEATURES), jnp.float32), -6.0, 6.0)
    return sample.astype(jnp.bfloat16)


def draw_key_vectors(key, part):
    key = jax.random.fold_in(key, 12)
    sample = jnp.clip(jax.random.normal(key, (NTT, NHT, ROWS, FEATURES), jnp.float32), -6.0, 6.0)
    return sample.astype(jnp.bfloat16)


def draw_out_grads(key, part):
    key = jax.random.fold_in(key, 13)
    column = jnp.arange(NTT * NHT).reshape(NTT, NHT).astype(jnp.float32) / max(NTT * NHT - 1, 1)
    head_rank = (jnp.arange(FEATURES) // HD).astype(jnp.float32) / max(FEATURES // HD - 1, 1)
    scaling = jnp.exp(math.log(3.0) * (column[:, :, None, None] + head_rank[None, None, None, :])) / 3.0
    sample = jnp.clip(jax.random.normal(key, (NTT, NHT, ROWS, FEATURES), jnp.float32), -3.0, 3.0) * scaling
    return jnp.clip(sample, -9.0, 9.0).astype(jnp.bfloat16)


def draw_query_gain(key, part):
    key = jax.random.fold_in(key, 21)
    sample = jax.random.uniform(key, (HD,), jnp.float32, 0.6, 2.4)
    return sample


def draw_key_gain(key, part):
    key = jax.random.fold_in(key, 22)
    sample = jax.random.uniform(key, (HD,), jnp.float32, 0.6, 2.4)
    return sample


def draw_frame_counts(key, part):
    key = jax.random.fold_in(key, 31)
    return padded_counts(key, NTT, TF)


def draw_row_counts(key, part):
    key = jax.random.fold_in(key, 32)
    return padded_counts(key, NHT, TH)


def level_of(key, extent, cuts, smallest, top_value):
    level, own = 1.0, jax.random.fold_in(key, 6)
    for axis_at, blocks in cuts:
        steps = jnp.exp(jax.random.uniform(jax.random.fold_in(own, axis_at), (blocks,), jnp.float32, smallest / len(cuts), top_value / len(cuts)))
        level = level * jnp.repeat(steps, extent[axis_at] // blocks).reshape([-1 if axis == axis_at else 1 for axis in range(len(extent))])
    return level


def gaussian(own_key, dims, scale, most, shards=(), kind=jnp.bfloat16):
    loudness = level_of(own_key, dims, shards, -0.22, 0.18) if shards else 1.0
    entries = jax.random.normal(own_key, dims, jnp.float32) * scale * loudness
    return jnp.minimum(jnp.maximum(entries, -most), most).astype(kind)


def setup_inputs(seed: int = 0) -> dict:
    arg_keys = jax.random.split(jax.random.key(seed), 9)
    queries = draw_queries(jax.random.fold_in(arg_keys[8], 71), 0)
    key_vectors = draw_key_vectors(jax.random.fold_in(arg_keys[8], 71), 0)
    value_vectors = gaussian(arg_keys[2], (NTT, NHT, ROWS, FEATURES), 1.0, 6.0, ((0, 8), (1, 4), (3, 8)))
    out_grads = draw_out_grads(jax.random.fold_in(arg_keys[8], 71), 0)
    query_gain = draw_query_gain(jax.random.fold_in(arg_keys[8], 71), 0)
    key_gain = draw_key_gain(jax.random.fold_in(arg_keys[8], 71), 0)
    frame_counts = draw_frame_counts(jax.random.fold_in(arg_keys[8], 71), 0)
    row_counts = draw_row_counts(jax.random.fold_in(arg_keys[8], 71), 0)
    return dict(queries=queries, key_vectors=key_vectors, value_vectors=value_vectors, out_grads=out_grads, query_gain=query_gain, key_gain=key_gain, frame_counts=frame_counts, row_counts=row_counts)


NORM_EPSILON = 1e-06

def pick(table, index):
    return jnp.sum(jnp.where(jnp.arange(table.shape[0], dtype=jnp.int32) == index, table, 0))

def head_norm(raw_values, norm_gain):
    leading = raw_values.shape[:-1]
    head_total = raw_values.shape[-1] // HD
    shaped = raw_values.astype(jnp.float32).reshape(leading + (head_total, HD))
    rms_inverse = lax.rsqrt(lax.optimization_barrier(jnp.mean(shaped * shaped, axis=-1, keepdims=True)) + NORM_EPSILON)
    unit_part = shaped * rms_inverse
    normed = (unit_part * norm_gain).astype(jnp.bfloat16).reshape(raw_values.shape)
    return (normed, unit_part, rms_inverse)

def norm_backward(grad_normed, unit_part, rms_inverse, norm_gain):
    shaped = grad_normed.reshape(unit_part.shape) * norm_gain
    inner = lax.optimization_barrier(jnp.mean(shaped * unit_part, axis=-1, keepdims=True))
    return (rms_inverse * (shaped - unit_part * inner)).reshape(grad_normed.shape)

def gain_term(grad_normed, unit_part):
    product = grad_normed.reshape(unit_part.shape) * unit_part
    return lax.optimization_barrier(jnp.sum(product.reshape(-1, HD), axis=0))

def neighbours(time_pos, height_pos, time_count, height_count, frame_counts, row_counts):
    present, frame_limits, row_limits, time_source, height_source = ([], [], [], [], [])
    for time_step in (-1, 0, 1):
        for height_step in (-1, 0, 1):
            time_at = time_pos + time_step
            height_at = height_pos + height_step
            present.append((time_at >= 0) & (time_at < time_count) & (height_at >= 0) & (height_at < height_count))
            time_near = jnp.clip(time_at, 0, time_count - 1).astype(jnp.int32)
            height_near = jnp.clip(height_at, 0, height_count - 1).astype(jnp.int32)
            frame_limits.append(pick(frame_counts, time_near))
            row_limits.append(pick(row_counts, height_near))
            time_source.append(time_near)
            height_source.append(height_near)
    return (jnp.stack(present), jnp.stack(frame_limits), jnp.stack(row_limits), time_source, height_source)

def key_mask(present, frame_limits, row_limits):
    positions = jnp.arange(TF * TH * TW, dtype=jnp.int32)
    frame_pos = positions // (TH * TW)
    row_pos = positions % (TH * TW) // TW
    allowed = present[:, None] & (frame_pos[None, :] < frame_limits[:, None]) & (row_pos[None, :] < row_limits[:, None])
    return allowed.reshape(-1)

def tile_backward(query_rows, key_rows, value_rows, grad_rows, allowed):
    row_count = query_rows.shape[0]
    feature_count = query_rows.shape[1]
    scaling = 1.0 / math.sqrt(HD)
    zeros_query = jnp.zeros((row_count, feature_count), jnp.float32)
    zeros_keys = jnp.zeros((key_rows.shape[0], feature_count), jnp.float32)

    def head_step(head_index, running):
        query_grad, key_grad, value_grad = running
        head_start = head_index * HD
        q_head = lax.dynamic_slice_in_dim(query_rows, head_start, HD, 1)
        k_head = lax.dynamic_slice_in_dim(key_rows, head_start, HD, 1)
        v_head = lax.dynamic_slice_in_dim(value_rows, head_start, HD, 1)
        g_head = lax.dynamic_slice_in_dim(grad_rows, head_start, HD, 1)
        scores = jnp.dot(q_head, k_head.T, preferred_element_type=jnp.float32) * scaling
        masked = jnp.where(allowed[None, :], scores, -1e+30)
        row_max = lax.optimization_barrier(jnp.max(masked, axis=1, keepdims=True))
        exponent = jnp.where(allowed[None, :], jnp.exp(masked - row_max), 0.0)
        weights = exponent / lax.optimization_barrier(jnp.sum(exponent, axis=1, keepdims=True))
        weights_low = weights.astype(jnp.bfloat16)
        attn_out = jnp.dot(weights_low, v_head, preferred_element_type=jnp.float32)
        row_delta = lax.optimization_barrier(jnp.sum(g_head.astype(jnp.float32) * attn_out, axis=1, keepdims=True))
        weight_grad = jnp.dot(g_head, v_head.T, preferred_element_type=jnp.float32)
        score_grad = (weights * (weight_grad - row_delta) * scaling).astype(jnp.bfloat16)
        query_grad = lax.dynamic_update_slice_in_dim(query_grad, jnp.dot(score_grad, k_head, preferred_element_type=jnp.float32), head_start, 1)
        key_grad = lax.dynamic_update_slice_in_dim(key_grad, jnp.dot(score_grad.T, q_head, preferred_element_type=jnp.float32), head_start, 1)
        value_grad = lax.dynamic_update_slice_in_dim(value_grad, jnp.dot(weights_low.T, g_head, preferred_element_type=jnp.float32), head_start, 1)
        return (query_grad, key_grad, value_grad)
    return lax.fori_loop(0, feature_count // HD, head_step, (zeros_query, zeros_keys, zeros_keys))

def reference(queries, key_vectors, value_vectors, out_grads, query_gain, key_gain, frame_counts, row_counts):
    time_count, height_count, row_count, feature_count = queries.shape
    tile_size = TF * TH * TW
    width_tiles = row_count // tile_size
    q_normed, q_unit, q_inverse = head_norm(queries, query_gain)
    k_normed, k_unit, k_inverse = head_norm(key_vectors, key_gain)
    positions = jnp.arange(row_count, dtype=jnp.int32) % tile_size
    frame_pos = positions // (TH * TW)
    row_pos = positions % (TH * TW) // TW
    frame_valid = frame_pos[None, :] < frame_counts[:, None]
    row_valid = row_pos[None, :] < row_counts[:, None]
    query_valid = frame_valid[:, None, :] & row_valid[None, :, :]
    masked_grads = jnp.where(query_valid[..., None], out_grads, jnp.zeros_like(out_grads))

    def column_step(running, column):
        key_sums, value_sums = running
        time_pos = column // height_count
        height_pos = column % height_count
        present, frame_limits, row_limits, time_source, height_source = neighbours(time_pos, height_pos, time_count, height_count, frame_counts, row_counts)
        allowed = key_mask(present, frame_limits, row_limits)
        near_keys = jnp.stack([k_normed[time_source[index], height_source[index]] for index in range(9)])
        near_values = jnp.stack([value_vectors[time_source[index], height_source[index]] for index in range(9)])
        query_parts = []
        for width_index in range(width_tiles):
            lower = width_index * tile_size
            keys_here = near_keys[:, lower:lower + tile_size].reshape(9 * tile_size, feature_count)
            values_here = near_values[:, lower:lower + tile_size].reshape(9 * tile_size, feature_count)
            query_grad, key_grad, value_grad = tile_backward(q_normed[time_pos, height_pos, lower:lower + tile_size], keys_here, values_here, masked_grads[time_pos, height_pos, lower:lower + tile_size], allowed)
            key_low = lax.optimization_barrier(key_grad.astype(jnp.bfloat16)).astype(jnp.float32)
            value_low = lax.optimization_barrier(value_grad.astype(jnp.bfloat16)).astype(jnp.float32)
            for index in range(9):
                first = index * tile_size
                key_sums = key_sums.at[time_source[index], height_source[index], lower:lower + tile_size].add(key_low[first:first + tile_size])
                value_sums = value_sums.at[time_source[index], height_source[index], lower:lower + tile_size].add(value_low[first:first + tile_size])
            query_parts.append(query_grad)
        return ((key_sums, value_sums), jnp.concatenate(query_parts, axis=0))
    start = (jnp.zeros(queries.shape, jnp.float32), jnp.zeros(queries.shape, jnp.float32))
    finals, query_columns = lax.scan(column_step, start, jnp.arange(time_count * height_count, dtype=jnp.int32))
    key_sums, value_sums = finals
    dq_normed = query_columns.reshape(queries.shape)
    d_queries = norm_backward(dq_normed, q_unit, q_inverse, query_gain).astype(jnp.bfloat16)
    d_keys = norm_backward(key_sums, k_unit, k_inverse, key_gain).astype(jnp.bfloat16)
    d_values = value_sums.astype(jnp.bfloat16)
    head_total = feature_count // HD
    scaling = 1.0 / math.sqrt(time_count * height_count * row_count * head_total)
    gain_grads = jnp.stack([gain_term(dq_normed, q_unit), gain_term(key_sums, k_unit)]) * scaling
    return (d_queries, d_keys, d_values, gain_grads)
```

```python
import functools
import math

import jax
import jax.numpy as jnp
from jax import lax
from jax.experimental import pallas as pl
from jax.experimental.pallas import tpu as pltpu
from jax.sharding import PartitionSpec as P

HD = 128
TF = 6
TH = 8
TW = 8
TILE = TF * TH * TW
NORM_EPSILON = 1e-06
SCALE = 1.0 / math.sqrt(HD)
LOG2E = math.log2(math.e)
CHUNK = 128
STEPS = (-1, 0, 1)


def valid_rows(shape, frame_limit, row_limit):
    token = lax.broadcasted_iota(jnp.int32, shape, 0)
    return ((token >> 6) < frame_limit) & (((token >> 3) & 7) < row_limit)


def unit_norm(raw):
    wide = raw.astype(jnp.float32)
    inverse = lax.rsqrt(jnp.mean(wide * wide, axis=-1, keepdims=True) + NORM_EPSILON)
    return wide * inverse, inverse


def norm_back(grad, unit, inverse, gain):
    shaped = grad * gain
    inner = jnp.mean(shaped * unit, axis=-1, keepdims=True)
    return inverse * (shaped - unit * inner)


def fold(x, op):
    return op(x.reshape(x.shape[0] // 8, 8, x.shape[1]), axis=0)


def attention_kernel(limits, query_gain, key_gain, queries, grads, *rest):
    tiles, rest = rest[:9], rest[9:]
    terms, rest = rest[:9], rest[9:]
    d_queries, gains, kn, probs, dps = rest
    q_unit, q_inverse = unit_norm(queries[...])
    gain_q = query_gain[...]
    gain_k = key_gain[...]
    qn = (q_unit * gain_q).astype(jnp.bfloat16)
    gm = jnp.where(
        valid_rows((TILE, HD), limits[4], limits[13]), grads[...], jnp.zeros_like(grads[...])
    )
    qt = qn.T
    gt = gm.T
    order = (4, 1, 7, 3, 5, 0, 2, 6, 8)

    top = jnp.full((1, TILE), -1e30, jnp.float32)
    total = jnp.zeros((1, TILE), jnp.float32)
    tops = {}
    for j in order:
        unit, _ = unit_norm(tiles[j][0])
        normed = (unit * gain_k).astype(jnp.bfloat16)
        kn[j] = normed
        bias = jnp.where(valid_rows((TILE, HD), limits[j], limits[9 + j]), 0.0, -1e30)
        tile_top = jnp.full((8, TILE), -1e30, jnp.float32)
        for c in range(0, TILE, CHUNK):
            s = jnp.dot(normed[c : c + CHUNK], qt, preferred_element_type=jnp.float32)
            b = bias[c : c + CHUNK]
            s = s * (SCALE * LOG2E) + jnp.concatenate([b, b, b], axis=1)
            probs[j, c : c + CHUNK] = s
            tile_top = jnp.maximum(tile_top, fold(s, jnp.max))
        new_top = jnp.maximum(top, jnp.max(tile_top, axis=0, keepdims=True))
        part = jnp.zeros((8, TILE), jnp.float32)
        for c in range(0, TILE, CHUNK):
            e = jnp.exp2(probs[j, c : c + CHUNK] - new_top)
            probs[j, c : c + CHUNK] = e
            part = part + fold(e, jnp.sum)
        total = total * jnp.exp2(top - new_top) + jnp.sum(part, axis=0, keepdims=True)
        top = new_top
        tops[j] = new_top

    inverse_total = 1.0 / total
    delta8 = jnp.zeros((8, TILE), jnp.float32)
    for j in order:
        factor = jnp.exp2(tops[j] - top) * inverse_total
        lows = []
        for c in range(0, TILE, CHUNK):
            dp = jnp.dot(tiles[j][1, c : c + CHUNK], gt, preferred_element_type=jnp.float32)
            p = probs[j, c : c + CHUNK] * factor
            low = p.astype(jnp.bfloat16)
            probs[j, c : c + CHUNK] = p
            dps[j, c : c + CHUNK] = dp
            delta8 = delta8 + fold(low.astype(jnp.float32) * dp, jnp.sum)
            dv = jnp.dot(low, gm, preferred_element_type=jnp.float32)
            terms[j][1, c : c + CHUNK] = dv.astype(jnp.bfloat16)
    delta = jnp.sum(delta8, axis=0, keepdims=True)

    dq_t = jnp.zeros((HD, TILE), jnp.float32)
    key_gain_sum = jnp.zeros((8, HD), jnp.float32)
    for j in order:
        unit, _ = unit_norm(tiles[j][0])
        for c in range(0, TILE, CHUNK):
            ds = (probs[j, c : c + CHUNK] * (dps[j, c : c + CHUNK] - delta) * SCALE).astype(
                jnp.bfloat16
            )
            dk = jnp.dot(ds, qn, preferred_element_type=jnp.float32).astype(jnp.bfloat16)
            terms[j][0, c : c + CHUNK] = dk
            key_gain_sum = key_gain_sum + fold(
                dk.astype(jnp.float32) * unit[c : c + CHUNK], jnp.sum
            )
            dq_t = dq_t + lax.dot_general(
                kn[j, c : c + CHUNK],
                ds,
                (((0,), (0,)), ((), ())),
                preferred_element_type=jnp.float32,
            )
    dq = dq_t.T
    d_queries[...] = norm_back(dq, q_unit, q_inverse, gain_q).astype(jnp.bfloat16)

    @pl.when(pl.program_id(0) == 0)
    def _():
        gains[...] = jnp.zeros_like(gains)

    gains[0:8] += fold(dq * q_unit, jnp.sum)
    gains[8:16] += key_gain_sum


def attention(limits, query_gain, key_gain, queries, grads, tiles):
    heads = queries.shape[1] // HD
    row = pl.BlockSpec((TILE, HD), lambda h: (0, h))
    pair = pl.BlockSpec((2, TILE, HD), lambda h: (0, 0, h))
    whole = pl.BlockSpec((1, HD), lambda h: (0, 0))
    pair_shape = jax.ShapeDtypeStruct((2,) + queries.shape, jnp.bfloat16)
    outs = pl.pallas_call(
        attention_kernel,
        grid=(heads,),
        in_specs=[pl.BlockSpec(memory_space=pltpu.SMEM), whole, whole, row, row] + [pair] * 9,
        out_specs=[pair] * 9 + [row, pl.BlockSpec((16, HD), lambda h: (0, 0))],
        out_shape=[pair_shape] * 9
        + [
            jax.ShapeDtypeStruct(queries.shape, jnp.bfloat16),
            jax.ShapeDtypeStruct((16, HD), jnp.float32),
        ],
        scratch_shapes=[
            pltpu.VMEM((9, TILE, HD), jnp.bfloat16),
            pltpu.VMEM((9, TILE, TILE), jnp.float32),
            pltpu.VMEM((9, TILE, TILE), jnp.float32),
        ],
        compiler_params=pltpu.CompilerParams(vmem_limit_bytes=48 * 2**20),
        cost_estimate=pl.CostEstimate(
            flops=heads * 10 * TILE * TILE * 9 * HD,
            bytes_accessed=40 * TILE * queries.shape[1] * 2,
            transcendentals=heads * 9 * TILE * TILE,
        ),
    )(limits, query_gain[None], key_gain[None], queries, grads, *tiles)
    return outs[:9], outs[9], outs[10]


def finish_kernel(key_gain, keys, *rest):
    parts, (d_keys, d_values) = rest[:-2], rest[-2:]
    total = parts[0][...].astype(jnp.float32)
    for part in parts[1:]:
        total = total + part[...].astype(jnp.float32)
    unit, inverse = unit_norm(keys[...])
    d_keys[...] = norm_back(total[0], unit, inverse, key_gain[...]).astype(jnp.bfloat16)
    d_values[...] = total[1].astype(jnp.bfloat16)


def finish(key_gain, keys, parts):
    heads = keys.shape[1] // HD
    row = pl.BlockSpec((TILE, HD), lambda h: (0, h))
    pair = pl.BlockSpec((2, TILE, HD), lambda h: (0, 0, h))
    whole = pl.BlockSpec((1, HD), lambda h: (0, 0))
    return pl.pallas_call(
        finish_kernel,
        grid=(heads,),
        in_specs=[whole, row] + [pair] * len(parts),
        out_specs=[row, row],
        out_shape=[jax.ShapeDtypeStruct(keys.shape, jnp.bfloat16)] * 2,
        compiler_params=pltpu.CompilerParams(vmem_limit_bytes=16 * 2**20),
    )(key_gain[None], keys, *parts)


def shifted(block, axis, distance):
    devices = range(lax.axis_size(axis))
    route = [(i - distance, i) for i in devices if i - distance in devices]
    return lax.ppermute(block, axis, route)


def total_over(x, axes):
    for axis in axes:
        size = lax.axis_size(axis)
        bit = 1
        while bit < size:
            x = x + lax.ppermute(x, axis, [(i, i ^ bit) for i in range(size)])
            bit *= 2
    return x


def window_limits(frame_counts, row_counts):
    time_index = lax.axis_index("tm")
    height_index = lax.axis_index("height")
    time_count = frame_counts.shape[0]
    height_count = row_counts.shape[0]
    frames = jnp.concatenate([jnp.zeros(1, jnp.int32), frame_counts, jnp.zeros(1, jnp.int32)])
    rows = jnp.concatenate([jnp.zeros(1, jnp.int32), row_counts, jnp.zeros(1, jnp.int32)])
    near_frames = lax.dynamic_slice_in_dim(frames, time_index, 3)
    near_rows = lax.dynamic_slice_in_dim(rows, height_index, 3)
    return jnp.concatenate([jnp.repeat(near_frames, 3), jnp.tile(near_rows, 3)])


def on_device(
    queries, key_vectors, value_vectors, out_grads, query_gain, key_gain, frame_counts, row_counts
):
    time_count = lax.axis_size("tm")
    height_count = lax.axis_size("height")
    row_count = queries.shape[2]
    feature_count = queries.shape[3]
    keys = key_vectors[0, 0]
    own = jnp.stack([keys, value_vectors[0, 0]])
    limits = window_limits(frame_counts, row_counts)

    tiles = {(0, 0): own}
    for a in (-1, 1):
        tiles[a, 0] = shifted(own, "tm", -a)
    for b in (-1, 1):
        tiles[0, b] = shifted(own, "height", -b)
    for a in (-1, 1):
        for b in (-1, 1):
            tiles[a, b] = shifted(tiles[a, 0], "height", -b)

    outs, d_queries, gain_parts = attention(
        limits,
        query_gain,
        key_gain,
        queries[0, 0],
        out_grads[0, 0],
        [tiles[a, b] for a in STEPS for b in STEPS],
    )
    terms = {(a, b): outs[3 * (a + 1) + b + 1] for a in STEPS for b in STEPS}

    landed = {}
    for a in (-1, 1, 0):
        for b in (-1, 1):
            landed[a, b] = shifted(terms[a, b], "height", b)
    parts = [terms[0, 0], landed[0, -1], landed[0, 1]]
    for a in (-1, 1):
        side = (
            terms[a, 0].astype(jnp.float32)
            + landed[a, -1].astype(jnp.float32)
            + landed[a, 1].astype(jnp.float32)
        ).astype(jnp.bfloat16)
        parts.append(shifted(side, "tm", a))
    d_keys, d_values = finish(key_gain, keys, parts)

    gain_local = jnp.sum(gain_parts.reshape(2, 8, HD), axis=1)
    gain_total = total_over(gain_local, ("dp", "tm", "height"))
    head_total = lax.axis_size("dp") * (feature_count // HD)
    scaling = 1.0 / math.sqrt(time_count * height_count * row_count * head_total)
    gain_grads = gain_total * scaling
    return (d_queries[None, None], d_keys[None, None], d_values[None, None], gain_grads)


def solution(mesh):
    split = P("tm", "height", None, "dp")
    return jax.shard_map(
        on_device,
        mesh=mesh,
        in_specs=(split,) * 4 + (P(),) * 4,
        out_specs=(split,) * 3 + (P(),),
        check_vma=False,
    )
```

```python
import functools
import math

import jax
import jax.numpy as jnp
from jax import lax
from jax.experimental import pallas as pl
from jax.experimental.pallas import tpu as pltpu
from jax.sharding import PartitionSpec as P

HD = 128
TF = 6
TH = 8
TW = 8
TILE = TF * TH * TW
NORM_EPSILON = 1e-06
SCALE = 1.0 / math.sqrt(HD)
LOG2E = math.log2(math.e)
CHUNK = 128


def valid_rows(shape, frame_limit, row_limit):
    token = lax.broadcasted_iota(jnp.int32, shape, 0)
    return ((token >> 6) < frame_limit) & (((token >> 3) & 7) < row_limit)


def unit_norm(raw):
    wide = raw.astype(jnp.float32)
    inverse = lax.rsqrt(jnp.mean(wide * wide, axis=-1, keepdims=True) + NORM_EPSILON)
    return wide * inverse, inverse


def norm_back(grad, unit, inverse, gain):
    shaped = grad * gain
    inner = jnp.mean(shaped * unit, axis=-1, keepdims=True)
    return inverse * (shaped - unit * inner)


def fold(x, op):
    return op(x.reshape(x.shape[0] // 8, 8, x.shape[1]), axis=0)


def near(table, index):
    last = table.shape[0] - 1
    even = index % 2 == 0
    below = jnp.where(index == 0, 0, table[jnp.maximum(index - 1, 0)])
    above = jnp.where(index == last, 0, table[jnp.minimum(index + 1, last)])
    return table[index], jnp.where(even, above, below), jnp.where(even, below, above)


def attention_kernel(frame_counts, row_counts, query_gain, key_gain, queries, grads, *rest):
    ins, (own, h_even, h_odd, ce, te, co, to, x_even, x_odd, d_queries, gains), scratch = (
        rest[:14],
        rest[14:25],
        rest[25:],
    )
    keys, values, t_even, tk_odd, tv_odd, he, ho, c_even, c_odd, vx, zke, zko, zve, zvo = ins
    kn, probs, dps = scratch
    time_index = lax.axis_index("tm")
    across = (time_index == 3) | (time_index == 4)
    f, fe, fo = near(frame_counts, time_index)
    r, re, ro = near(row_counts, lax.axis_index("height"))
    frames = (f, fe, fo, f, f, fe, fe, fo, fo)
    rows = (r, r, r, re, ro, re, ro, re, ro)

    def pick_keys(j):
        if j in (7, 8):
            return jnp.where(across, {7: zke, 8: zko}[j][...], c_odd[j - 7, 0])
        if j in (0, 2):
            return {0: keys, 2: tk_odd}[j][...]
        return {1: t_even, 3: he, 4: ho, 5: c_even.at[0], 6: c_even.at[1]}[j][0]

    def pick_values(j):
        if j in (2, 7, 8):
            plain = tv_odd[...] if j == 2 else c_odd[j - 7, 1]
            return jnp.where(across, {2: vx, 7: zve, 8: zvo}[j][...], plain)
        if j == 0:
            return values[...]
        return {1: t_even, 3: he, 4: ho, 5: c_even.at[0], 6: c_even.at[1]}[j][1]

    targets = {
        0: (own,),
        1: (te,),
        2: (to,),
        3: (h_even,),
        4: (h_odd,),
        5: (ce.at[0],),
        6: (ce.at[1],),
        7: (co.at[0], x_even),
        8: (co.at[1], x_odd),
    }

    q_unit, q_inverse = unit_norm(queries[...])
    gain_q = query_gain[...]
    gain_k = key_gain[...]
    qn = (q_unit * gain_q).astype(jnp.bfloat16)
    gm = jnp.where(
        valid_rows((TILE, HD), f, r), grads[...], jnp.zeros_like(grads[...])
    )
    qt = qn.T
    gt = gm.T

    top = jnp.full((1, TILE), -1e30, jnp.float32)
    total = jnp.zeros((1, TILE), jnp.float32)
    tops = {}
    for j in range(9):
        unit, _ = unit_norm(pick_keys(j))
        normed = (unit * gain_k).astype(jnp.bfloat16)
        kn[j] = normed
        bias = jnp.where(valid_rows((TILE, HD), frames[j], rows[j]), 0.0, -1e30)
        tile_top = jnp.full((8, TILE), -1e30, jnp.float32)
        for c in range(0, TILE, CHUNK):
            s = jnp.dot(normed[c : c + CHUNK], qt, preferred_element_type=jnp.float32)
            b = bias[c : c + CHUNK]
            s = s * (SCALE * LOG2E) + jnp.concatenate([b, b, b], axis=1)
            probs[j, c : c + CHUNK] = s
            tile_top = jnp.maximum(tile_top, fold(s, jnp.max))
        new_top = jnp.maximum(top, jnp.max(tile_top, axis=0, keepdims=True))
        part = jnp.zeros((8, TILE), jnp.float32)
        for c in range(0, TILE, CHUNK):
            e = jnp.exp2(probs[j, c : c + CHUNK] - new_top)
            probs[j, c : c + CHUNK] = e
            part = part + fold(e, jnp.sum)
        total = total * jnp.exp2(top - new_top) + jnp.sum(part, axis=0, keepdims=True)
        top = new_top
        tops[j] = new_top

    inverse_total = 1.0 / total
    delta8 = jnp.zeros((8, TILE), jnp.float32)
    for j in range(9):
        factor = jnp.exp2(tops[j] - top) * inverse_total
        v = pick_values(j)
        for c in range(0, TILE, CHUNK):
            dp = jnp.dot(v[c : c + CHUNK], gt, preferred_element_type=jnp.float32)
            p = probs[j, c : c + CHUNK] * factor
            low = p.astype(jnp.bfloat16)
            probs[j, c : c + CHUNK] = p
            dps[j, c : c + CHUNK] = dp
            delta8 = delta8 + fold(low.astype(jnp.float32) * dp, jnp.sum)
            dv = jnp.dot(low, gm, preferred_element_type=jnp.float32).astype(jnp.bfloat16)
            for target in targets[j]:
                target[1, c : c + CHUNK] = dv
    delta = jnp.sum(delta8, axis=0, keepdims=True)

    dq_t = jnp.zeros((HD, TILE), jnp.float32)
    key_gain_sum = jnp.zeros((8, HD), jnp.float32)
    for j in range(9):
        unit, _ = unit_norm(pick_keys(j))
        for c in range(0, TILE, CHUNK):
            ds = (probs[j, c : c + CHUNK] * (dps[j, c : c + CHUNK] - delta) * SCALE).astype(
                jnp.bfloat16
            )
            dk = jnp.dot(ds, qn, preferred_element_type=jnp.float32).astype(jnp.bfloat16)
            for target in targets[j]:
                target[0, c : c + CHUNK] = dk
            key_gain_sum = key_gain_sum + fold(
                dk.astype(jnp.float32) * unit[c : c + CHUNK], jnp.sum
            )
            dq_t = dq_t + lax.dot_general(
                kn[j, c : c + CHUNK],
                ds,
                (((0,), (0,)), ((), ())),
                preferred_element_type=jnp.float32,
            )
    dq = dq_t.T
    d_queries[...] = norm_back(dq, q_unit, q_inverse, gain_q).astype(jnp.bfloat16)

    @pl.when(pl.program_id(0) == 0)
    def _():
        gains[...] = jnp.zeros_like(gains)

    gains[0:8] += fold(dq * q_unit, jnp.sum)
    gains[8:16] += key_gain_sum


def block_specs():
    row = pl.BlockSpec((TILE, HD), lambda h: (0, h))
    pair = pl.BlockSpec((2, TILE, HD), lambda h: (0, 0, h))
    quad = pl.BlockSpec((2, 2, TILE, HD), lambda h: (0, 0, 0, h))
    whole = pl.BlockSpec((1, HD), lambda h: (0, 0))
    return row, pair, quad, whole


def attention(frame_counts, row_counts, query_gain, key_gain, queries, grads, ins):
    heads = queries.shape[1] // HD
    row, pair, quad, whole = block_specs()
    spec_of = {2: row, 3: pair, 4: quad}
    low = lambda *lead: jax.ShapeDtypeStruct(lead + queries.shape, jnp.bfloat16)
    return pl.pallas_call(
        attention_kernel,
        grid=(heads,),
        in_specs=[pl.BlockSpec(memory_space=pltpu.SMEM)] * 2
        + [whole, whole, row, row]
        + [spec_of[x.ndim] for x in ins],
        out_specs=[pair, pair, pair, quad, pair, quad, pair, pair, pair, row]
        + [pl.BlockSpec((16, HD), lambda h: (0, 0))],
        out_shape=[low(2), low(2), low(2), low(2, 2), low(2), low(2, 2), low(2)]
        + [low(2), low(2), low()]
        + [jax.ShapeDtypeStruct((16, HD), jnp.float32)],
        scratch_shapes=[
            pltpu.VMEM((9, TILE, HD), jnp.bfloat16),
            pltpu.VMEM((9, TILE, TILE), jnp.float32),
            pltpu.VMEM((9, TILE, TILE), jnp.float32),
        ],
        compiler_params=pltpu.CompilerParams(vmem_limit_bytes=36 * 2**20),
        cost_estimate=pl.CostEstimate(
            flops=heads * 10 * TILE * TILE * 9 * HD,
            bytes_accessed=40 * TILE * queries.shape[1] * 2,
            transcendentals=heads * 9 * TILE * TILE,
        ),
    )(frame_counts, row_counts, query_gain[None], key_gain[None], queries, grads, *ins)


def finish_kernel(key_gain, keys, *rest):
    pairs, (tk, tv, vx, d_keys, d_values) = rest[:-5], rest[-5:]
    dk = tk[...].astype(jnp.float32)
    time_index = lax.axis_index("tm")
    dv = jnp.where((time_index == 3) | (time_index == 4), vx[...], tv[...])
    dv = jnp.where((time_index == 0) | (time_index == 7), 0.0, dv.astype(jnp.float32))
    for part in pairs:
        dk = dk + part[0].astype(jnp.float32)
        dv = dv + part[1].astype(jnp.float32)
    unit, inverse = unit_norm(keys[...])
    d_keys[...] = norm_back(dk, unit, inverse, key_gain[...]).astype(jnp.bfloat16)
    d_values[...] = dv.astype(jnp.bfloat16)


def finish(key_gain, keys, pairs, rows):
    heads = keys.shape[1] // HD
    row, pair, _, whole = block_specs()
    return pl.pallas_call(
        finish_kernel,
        grid=(heads,),
        in_specs=[whole, row] + [pair] * len(pairs) + [row] * len(rows),
        out_specs=[row, row],
        out_shape=[jax.ShapeDtypeStruct(keys.shape, jnp.bfloat16)] * 2,
        compiler_params=pltpu.CompilerParams(vmem_limit_bytes=16 * 2**20),
    )(key_gain[None], keys, *pairs, *rows)


def swaps(size, first, skip=()):
    route = []
    for i in range(first, size - 1, 2):
        if i not in skip:
            route += [(i, i + 1), (i + 1, i)]
    return route


def total_over(x, axes):
    for axis in axes:
        size = lax.axis_size(axis)
        bit = 1
        while bit < size:
            x = x + lax.ppermute(x, axis, [(i, i ^ bit) for i in range(size)])
            bit *= 2
    return x


def on_device(
    queries, key_vectors, value_vectors, out_grads, query_gain, key_gain, frame_counts, row_counts
):
    time_count = lax.axis_size("tm")
    height_count = lax.axis_size("height")
    row_count = queries.shape[2]
    feature_count = queries.shape[3]
    keys = key_vectors[0, 0]
    values = value_vectors[0, 0]

    even_t, odd_t = swaps(8, 0), swaps(8, 1, (3,))
    even_h, odd_h = swaps(4, 0), swaps(4, 1)
    key_route = odd_t + [(3, 4), (4, 3)]
    value_route = odd_t + [(3, 0), (4, 7)]
    arrive = [(0, 4), (7, 3)]
    far_even = [(4 * t + i, 4 * t + j) for t in (3, 4) for i, j in even_h]
    far_odd = [(4 * t + i, 4 * t + j) for t in (3, 4) for i, j in odd_h]
    both = ("tm", "height")

    tv = lax.ppermute(values, "tm", value_route)
    tk = lax.ppermute(keys, "tm", key_route)
    own = jnp.stack([keys, values])
    he = lax.ppermute(own, "height", even_h)
    ho = lax.ppermute(own, "height", odd_h)
    te = lax.ppermute(own, "tm", even_t)
    he, ho, te, tv = lax.optimization_barrier((he, ho, te, tv))
    vx = lax.ppermute(tv, "tm", arrive)
    sides = jnp.stack([he, ho])
    ce = lax.ppermute(sides, "tm", even_t)
    sides, tk = lax.optimization_barrier((sides, tk))
    co = lax.ppermute(sides, "tm", odd_t)
    zke = lax.ppermute(tk, both, far_even)
    zko = lax.ppermute(tk, both, far_odd)
    zve = lax.ppermute(vx, both, far_even)
    zvo = lax.ppermute(vx, both, far_odd)

    outs = attention(
        frame_counts,
        row_counts,
        query_gain,
        key_gain,
        queries[0, 0],
        out_grads[0, 0],
        [keys, values, te, tk, tv, he, ho, ce, co, vx, zke, zko, zve, zvo],
    )
    own, he, ho, ce, te, co, to, x_even, x_odd, d_queries, gain_parts = outs

    wide = lambda x: x.astype(jnp.float32)
    xe = lax.ppermute(x_even, both, far_even)
    xo = lax.ppermute(x_odd, both, far_odd)
    ce = lax.ppermute(ce, "tm", even_t)
    co = lax.ppermute(co, "tm", odd_t)
    gain_parts, _ = lax.optimization_barrier((gain_parts, x_odd))
    gain_local = total_over(jnp.sum(gain_parts.reshape(2, 8, HD), axis=1), ("dp",))
    gain_local, xe, xo = lax.optimization_barrier((gain_local, xe, xo))
    to = (wide(to) + wide(xe) + wide(xo)).astype(jnp.bfloat16)
    tv = lax.ppermute(to[1], "tm", value_route)
    tk = lax.ppermute(to[0], "tm", key_route)
    vx = lax.ppermute(tv, "tm", arrive)
    he = (wide(he) + wide(ce[0]) + wide(co[0])).astype(jnp.bfloat16)
    ho = (wide(ho) + wide(ce[1]) + wide(co[1])).astype(jnp.bfloat16)
    te, he, ho = lax.optimization_barrier((te, he, ho))
    he = lax.ppermute(he, "height", even_h)
    ho = lax.ppermute(ho, "height", odd_h)
    te = lax.ppermute(te, "tm", even_t)
    gain_local, te = lax.optimization_barrier((gain_local, te))
    gain_total = total_over(gain_local, ("tm", "height"))
    d_keys, d_values = finish(key_gain, keys, [own, te, he, ho], [tk, tv, vx])

    head_total = lax.axis_size("dp") * (feature_count // HD)
    scaling = 1.0 / math.sqrt(time_count * height_count * row_count * head_total)
    gain_grads = gain_total * scaling
    return (d_queries[None, None], d_keys[None, None], d_values[None, None], gain_grads)


def solution(mesh):
    split = P("tm", "height", None, "dp")
    return jax.shard_map(
        on_device,
        mesh=mesh,
        in_specs=(split,) * 4 + (P(),) * 4,
        out_specs=(split,) * 3 + (P(),),
        check_vma=False,
    )
```

```python
import functools
import math

import jax
import jax.numpy as jnp
from jax import lax
from jax.experimental import pallas as pl
from jax.experimental.pallas import tpu as pltpu
from jax.sharding import PartitionSpec as P

HD = 128
TF = 6
TH = 8
TW = 8
TILE = TF * TH * TW
NORM_EPSILON = 1e-06
SCALE = 1.0 / math.sqrt(HD)
LOG2E = math.log2(math.e)
ROOM = 9 * TILE + 256


def below(shape, count):
    return lax.broadcasted_iota(jnp.int32, shape, 0) < count


def pack_rows(held, block, rows):
    held[...] = jnp.zeros_like(held)
    for frame in range(TF):
        first = pl.multiple_of(frame * rows * TW, TW)
        held[pl.ds(first, TH * TW)] = block[frame * TH * TW : (frame + 1) * TH * TW]


def unpack_rows(out, held, frames, rows):
    for frame in range(TF):
        first = pl.multiple_of(frame * rows * TW, TW)
        block = held[pl.ds(first, TH * TW)]
        keep = below(block.shape, jnp.where(frame < frames, rows * TW, 0))
        out[frame * TH * TW : (frame + 1) * TH * TW] = jnp.where(keep, block, 0.0).astype(out.dtype)


def unit_norm(raw):
    wide = raw.astype(jnp.float32)
    inverse = lax.rsqrt(jnp.mean(wide * wide, axis=-1, keepdims=True) + NORM_EPSILON)
    return wide * inverse, inverse


def norm_back(grad, unit, inverse, gain):
    shaped = grad * gain
    inner = jnp.mean(shaped * unit, axis=-1, keepdims=True)
    return inverse * (shaped - unit * inner)


def fold(x, op):
    return op(x.reshape(x.shape[0] // 8, 8, x.shape[1]), axis=0)


def near(table, index):
    last = table.shape[0] - 1
    even = index % 2 == 0
    below = jnp.where(index == 0, 0, table[jnp.maximum(index - 1, 0)])
    above = jnp.where(index == last, 0, table[jnp.minimum(index + 1, last)])
    return table[index], jnp.where(even, above, below), jnp.where(even, below, above)


def attention_kernel(frame_counts, row_counts, query_gain, key_gain, queries, grads, *rest):
    ins, outs, scratch = rest[:14], rest[14:25], rest[25:]
    keys, values, t_even, tk, tv, h_even, h_odd, ck_even, ck_odd, cv_even, cv_odd = ins[:11]
    vx, zv_even, zv_odd = ins[11:]
    own, he, ho, te, to, cke, cko, cze, czo, d_queries, gains = outs
    kn, vs, bias, units, grads_kv, probs, dps, wide = scratch
    time_index = lax.axis_index("tm")
    across = (time_index == 3) | (time_index == 4)
    f, fe, fo = near(frame_counts, time_index)
    r, re, ro = near(row_counts, lax.axis_index("height"))
    frames = (f, fe, fo, f, f, fe, fe, fo, fo)
    rows = (r, r, r, re, ro, re, ro, re, ro)
    counts = [x * y * TW for x, y in zip(frames, rows)]
    key_refs = (
        keys, t_even.at[0], tk, h_even.at[0], h_odd.at[0],
        ck_even.at[0], ck_even.at[1], ck_odd.at[0], ck_odd.at[1],
    )
    value_refs = (
        values, t_even.at[1], tv, h_even.at[1], h_odd.at[1],
        cv_even.at[0], cv_odd.at[0], cv_even.at[1], cv_odd.at[1],
    )
    far_keys = {7: cv_even.at[1], 8: cv_odd.at[1]}
    far_values = {2: vx, 7: zv_even, 8: zv_odd}

    def pick(refs, far, j):
        near_by = refs[j][...]
        return jnp.where(across, far[j][...], near_by) if j in far else near_by

    def pick_keys(j):
        return pick(key_refs, far_keys, j)

    def pick_values(j):
        return pick(value_refs, far_values, j)

    key_targets = (
        (own.at[0],), (te.at[0],), (to.at[0],), (he.at[0],), (ho.at[0],),
        (cke.at[0],), (cke.at[1],), (cko.at[0], cze.at[2]), (cko.at[1], czo.at[2]),
    )
    value_targets = (
        own.at[1], te.at[1], to.at[1], he.at[1], ho.at[1],
        cze.at[0], czo.at[0], cze.at[1], czo.at[1],
    )

    q_unit, q_inverse = unit_norm(queries[...])
    gain_q = query_gain[...]
    gain_k = key_gain[...]
    qn = (q_unit * gain_q).astype(jnp.bfloat16)
    low_grads = grads[...]
    gm = jnp.where(below((TILE, HD), counts[0]), low_grads, jnp.zeros_like(low_grads))

    starts = [jnp.int32(0)]
    for j in range(9):
        at = pl.ds(pl.multiple_of(starts[j], HD), TILE)
        unit, _ = unit_norm(pick_keys(j))
        units[at] = unit
        kn[at] = (unit * gain_k).astype(jnp.bfloat16)
        vs[at] = pick_values(j)
        bias[at] = jnp.where(below((TILE, HD), counts[j]), 0.0, -1e30)
        starts.append(starts[j] + ((counts[j] + HD - 1) >> 7) * HD)
    at = pl.ds(pl.multiple_of(starts[9], HD), 256)
    kn[at] = jnp.zeros((256, HD), jnp.bfloat16)
    vs[at] = jnp.zeros((256, HD), jnp.bfloat16)
    bias[at] = jnp.full((256, HD), -1e30, jnp.float32)
    groups = lax.div((starts[9] >> 7) + 2, jnp.int32(3))
    wide[...] = jnp.zeros_like(wide)

    def attend(width):
        qs, gs = qn[:width], gm[:width]
        qt, gt = qs.T, gs.T

        def rows_of(i):
            return pl.ds(pl.multiple_of(i * TILE, HD), TILE)

        def score(i, top):
            s = jnp.dot(kn[rows_of(i)], qt, preferred_element_type=jnp.float32)
            b = bias[rows_of(i)]
            s = s * (SCALE * LOG2E) + jnp.concatenate([b] * (width // HD), axis=1)
            probs[rows_of(i), :width] = s
            return jnp.maximum(top, fold(s, jnp.max))

        top = lax.fori_loop(0, groups, score, jnp.full((8, width), -1e30, jnp.float32))
        top = jnp.max(top, axis=0, keepdims=True)

        def power(i, total):
            e = jnp.exp2(probs[rows_of(i), :width] - top)
            probs[rows_of(i), :width] = e
            return total + fold(e, jnp.sum)

        total = lax.fori_loop(0, groups, power, jnp.zeros((8, width), jnp.float32))
        inverse = 1.0 / jnp.sum(total, axis=0, keepdims=True)

        def weigh(i, delta):
            dp = jnp.dot(vs[rows_of(i)], gt, preferred_element_type=jnp.float32)
            p = probs[rows_of(i), :width] * inverse
            low = p.astype(jnp.bfloat16)
            probs[rows_of(i), :width] = p
            dps[rows_of(i), :width] = dp
            dv = jnp.dot(low, gs, preferred_element_type=jnp.float32)
            grads_kv[1, rows_of(i)] = dv.astype(jnp.bfloat16)
            return delta + fold(low.astype(jnp.float32) * dp, jnp.sum)

        delta = lax.fori_loop(0, groups, weigh, jnp.zeros((8, width), jnp.float32))
        delta = jnp.sum(delta, axis=0, keepdims=True)

        def back(i, dq_t):
            ds = probs[rows_of(i), :width] * (dps[rows_of(i), :width] - delta) * SCALE
            ds = ds.astype(jnp.bfloat16)
            dk = jnp.dot(ds, qs, preferred_element_type=jnp.float32)
            grads_kv[0, rows_of(i)] = dk.astype(jnp.bfloat16)
            return dq_t + lax.dot_general(
                kn[rows_of(i)], ds, (((0,), (0,)), ((), ())), preferred_element_type=jnp.float32
            )

        dq_t = lax.fori_loop(0, groups, back, jnp.zeros((HD, width), jnp.float32))
        wide[:width] = dq_t.T

    for width in (HD, 2 * HD, 3 * HD):
        pl.when((counts[0] > width - HD) & (counts[0] <= width))(functools.partial(attend, width))

    key_gain_sum = jnp.zeros((8, HD), jnp.float32)
    for j in range(9):
        at = pl.ds(pl.multiple_of(starts[j], HD), TILE)
        keep = below((TILE, HD), counts[j])
        zero = jnp.zeros((TILE, HD), jnp.bfloat16)
        dk = jnp.where(keep, grads_kv[0, at], zero)
        for target in key_targets[j]:
            target[...] = dk
        value_targets[j][...] = jnp.where(keep, grads_kv[1, at], zero)
        key_gain_sum = key_gain_sum + fold(dk.astype(jnp.float32) * units[at], jnp.sum)

    dq = wide[...]
    query_gain_sum = fold(dq * q_unit, jnp.sum)
    wide[...] = norm_back(dq, q_unit, q_inverse, gain_q)
    unpack_rows(d_queries, wide, f, r)

    @pl.when(pl.program_id(0) == 0)
    def _():
        gains[...] = jnp.zeros_like(gains)

    gains[0:8] += query_gain_sum
    gains[8:16] += key_gain_sum


def pack_kernel(row_counts, *refs):
    ins, (own, *outs, held) = refs[:4], refs[4:]
    rows = row_counts[lax.axis_index("height")]
    for i, (block, out) in enumerate(zip(ins, outs)):
        pack_rows(held, block[...].astype(jnp.float32), rows)
        packed = held[...].astype(out.dtype)
        out[...] = packed
        if i < 2:
            own[i] = packed


def pack(row_counts, *arrays):
    shape = arrays[0].shape
    heads = shape[1] // HD
    row, pair, _ = block_specs()
    return pl.pallas_call(
        pack_kernel,
        grid=(heads,),
        in_specs=[pl.BlockSpec(memory_space=pltpu.SMEM)] + [row] * 4,
        out_specs=[pair] + [row] * 4,
        out_shape=[jax.ShapeDtypeStruct((2,) + shape, jnp.bfloat16)]
        + [jax.ShapeDtypeStruct(shape, jnp.bfloat16)] * 4,
        scratch_shapes=[pltpu.VMEM((TILE, HD), jnp.float32)],
        compiler_params=pltpu.CompilerParams(vmem_limit_bytes=16 * 2**20),
    )(row_counts, *arrays)


def block_specs():
    row = pl.BlockSpec((TILE, HD), lambda h: (0, h))
    pair = pl.BlockSpec((2, TILE, HD), lambda h: (0, 0, h))
    whole = pl.BlockSpec((1, HD), lambda h: (0, 0))
    return row, pair, whole


def attention(frame_counts, row_counts, query_gain, key_gain, queries, grads, ins):
    heads = queries.shape[1] // HD
    row, pair, whole = block_specs()
    spec_of = {2: row, 3: pair}
    low = lambda *lead: jax.ShapeDtypeStruct(lead + queries.shape, jnp.bfloat16)
    return pl.pallas_call(
        attention_kernel,
        grid=(heads,),
        in_specs=[pl.BlockSpec(memory_space=pltpu.SMEM)] * 2
        + [whole, whole, row, row]
        + [spec_of[x.ndim] for x in ins],
        out_specs=[pair] * 7
        + [pl.BlockSpec((3, TILE, HD), lambda h: (0, 0, h))] * 2
        + [row, pl.BlockSpec((16, HD), lambda h: (0, 0))],
        out_shape=[low(2)] * 7
        + [low(3)] * 2
        + [low(), jax.ShapeDtypeStruct((16, HD), jnp.float32)],
        scratch_shapes=[
            pltpu.VMEM((ROOM, HD), jnp.bfloat16),
            pltpu.VMEM((ROOM, HD), jnp.bfloat16),
            pltpu.VMEM((ROOM, HD), jnp.float32),
            pltpu.VMEM((ROOM, HD), jnp.float32),
            pltpu.VMEM((2, ROOM, HD), jnp.bfloat16),
            pltpu.VMEM((ROOM, TILE), jnp.float32),
            pltpu.VMEM((ROOM, TILE), jnp.float32),
            pltpu.VMEM((TILE, HD), jnp.float32),
        ],
        compiler_params=pltpu.CompilerParams(vmem_limit_bytes=40 * 2**20),
        cost_estimate=pl.CostEstimate(
            flops=heads * 10 * TILE * TILE * 9 * HD,
            bytes_accessed=40 * TILE * queries.shape[1] * 2,
            transcendentals=heads * 9 * TILE * TILE,
        ),
    )(frame_counts, row_counts, query_gain[None], key_gain[None], queries, grads, *ins)


def finish_kernel(frame_counts, row_counts, key_gain, keys, *rest):
    pairs, (tk, tv, vx, d_keys, d_values, held) = rest[:-6], rest[-6:]
    dk = tk[...].astype(jnp.float32)
    time_index = lax.axis_index("tm")
    dv = jnp.where((time_index == 3) | (time_index == 4), vx[...], tv[...])
    dv = jnp.where((time_index == 0) | (time_index == 7), 0.0, dv.astype(jnp.float32))
    for part in pairs:
        dk = dk + part[0].astype(jnp.float32)
        dv = dv + part[1].astype(jnp.float32)
    unit, inverse = unit_norm(keys[...])
    frames, rows = frame_counts[time_index], row_counts[lax.axis_index("height")]
    held[...] = norm_back(dk, unit, inverse, key_gain[...])
    unpack_rows(d_keys, held, frames, rows)
    held[...] = dv
    unpack_rows(d_values, held, frames, rows)


def finish(frame_counts, row_counts, key_gain, keys, pairs, rows):
    heads = keys.shape[1] // HD
    row, pair, whole = block_specs()
    return pl.pallas_call(
        finish_kernel,
        grid=(heads,),
        in_specs=[pl.BlockSpec(memory_space=pltpu.SMEM)] * 2
        + [whole, row]
        + [pair] * len(pairs)
        + [row] * len(rows),
        out_specs=[row, row],
        out_shape=[jax.ShapeDtypeStruct(keys.shape, jnp.bfloat16)] * 2,
        scratch_shapes=[pltpu.VMEM((TILE, HD), jnp.float32)],
        compiler_params=pltpu.CompilerParams(vmem_limit_bytes=16 * 2**20),
    )(frame_counts, row_counts, key_gain[None], keys, *pairs, *rows)


def swaps(size, first, skip=()):
    route = []
    for i in range(first, size - 1, 2):
        if i not in skip:
            route += [(i, i + 1), (i + 1, i)]
    return route


def total_over(x, axes):
    for axis in axes:
        size = lax.axis_size(axis)
        bit = 1
        while bit < size:
            x = x + lax.ppermute(x, axis, [(i, i ^ bit) for i in range(size)])
            bit *= 2
    return x


def on_device(
    queries, key_vectors, value_vectors, out_grads, query_gain, key_gain, frame_counts, row_counts
):
    time_count = lax.axis_size("tm")
    height_count = lax.axis_size("height")
    row_count = queries.shape[2]
    feature_count = queries.shape[3]
    own, keys, values, packed_queries, grads = pack(
        row_counts, key_vectors[0, 0], value_vectors[0, 0], queries[0, 0], out_grads[0, 0]
    )

    even_t, odd_t = swaps(8, 0), swaps(8, 1, (3,))
    even_h, odd_h = swaps(4, 0), swaps(4, 1)
    key_route = odd_t + [(3, 4), (4, 3)]
    value_route = odd_t + [(3, 0), (4, 7)]
    arrive = [(0, 4), (7, 3)]
    time_index = lax.axis_index("tm")
    across = (time_index == 3) | (time_index == 4)
    far_even = [(4 * t + i, 4 * t + j) for t in (3, 4) for i, j in even_h]
    far_odd = [(4 * t + i, 4 * t + j) for t in (3, 4) for i, j in odd_h]
    both = ("tm", "height")

    tv = lax.ppermute(values, "tm", value_route)
    tk = lax.ppermute(keys, "tm", key_route)
    he = lax.ppermute(own, "height", even_h)
    ho = lax.ppermute(own, "height", odd_h)
    te = lax.ppermute(own, "tm", even_t)
    vx = lax.ppermute(tv, "tm", arrive)
    corner_keys = jnp.stack([he[0], ho[0]])
    tk, corner_keys = lax.optimization_barrier((tk, corner_keys))
    corner_values = jnp.stack([te[1], jnp.where(across, tk, tv)])
    cke = lax.ppermute(corner_keys, "tm", even_t)
    cko = lax.ppermute(corner_keys, "tm", odd_t)
    cve = lax.ppermute(corner_values, "height", even_h)
    cvo = lax.ppermute(corner_values, "height", odd_h)
    zve = lax.ppermute(vx, both, far_even)
    zvo = lax.ppermute(vx, both, far_odd)

    outs = attention(
        frame_counts,
        row_counts,
        query_gain,
        key_gain,
        packed_queries,
        grads,
        [keys, values, te, tk, tv, he, ho, cke, cko, cve, cvo, vx, zve, zvo],
    )
    own, he, ho, te, to, cke, cko, cze, czo, d_queries, gain_parts = outs

    def add(*parts):
        return sum(x.astype(jnp.float32) for x in parts).astype(jnp.bfloat16)

    cze = lax.ppermute(cze, "height", even_h)
    czo = lax.ppermute(czo, "height", odd_h)
    cke = lax.ppermute(cke, "tm", even_t)
    cko = lax.ppermute(cko, "tm", odd_t)
    gain_local = total_over(jnp.sum(gain_parts.reshape(2, 8, HD), axis=1), ("dp",))
    gain_local, cze, czo = lax.optimization_barrier((gain_local, cze, czo))
    far = jnp.where(across, cze[2].astype(jnp.float32) + czo[2].astype(jnp.float32), 0.0)
    tv = lax.ppermute(add(to[1], cze[1], czo[1]), "tm", value_route)
    tk = lax.ppermute(add(to[0], far), "tm", key_route)
    vx = lax.ppermute(tv, "tm", arrive)
    te = jnp.stack([te[0], add(te[1], cze[0], czo[0])])
    te = lax.ppermute(te, "tm", even_t)
    he = jnp.stack([add(he[0], cke[0], cko[0]), he[1]])
    ho = jnp.stack([add(ho[0], cke[1], cko[1]), ho[1]])
    he = lax.ppermute(he, "height", even_h)
    ho = lax.ppermute(ho, "height", odd_h)
    gain_local, tv, tk = lax.optimization_barrier((gain_local, tv, tk))
    gain_total = total_over(gain_local, ("tm", "height"))
    d_keys, d_values = finish(frame_counts, row_counts, key_gain, keys, [own, te, he, ho], [tk, tv, vx])

    head_total = lax.axis_size("dp") * (feature_count // HD)
    scaling = 1.0 / math.sqrt(time_count * height_count * row_count * head_total)
    gain_grads = gain_total * scaling
    return (d_queries[None, None], d_keys[None, None], d_values[None, None], gain_grads)


def solution(mesh):
    split = P("tm", "height", None, "dp")
    return jax.shard_map(
        on_device,
        mesh=mesh,
        in_specs=(split,) * 4 + (P(),) * 4,
        out_specs=(split,) * 3 + (P(),),
        check_vma=False,
    )
```

```python
import functools
import math

import jax
import jax.numpy as jnp
from jax import lax
from jax.experimental import pallas as pl
from jax.experimental.pallas import tpu as pltpu
from jax.sharding import PartitionSpec as P

HD = 128
TF = 6
TH = 8
TW = 8
TILE = TF * TH * TW
NORM_EPSILON = 1e-06
SCALE = 1.0 / math.sqrt(HD)
LOG2E = math.log2(math.e)
CHUNK = 384


def valid_rows(shape, frame_limit, row_limit):
    token = lax.broadcasted_iota(jnp.int32, shape, 0)
    return ((token >> 6) < frame_limit) & (((token >> 3) & 7) < row_limit)


def unit_norm(raw):
    wide = raw.astype(jnp.float32)
    inverse = lax.rsqrt(jnp.mean(wide * wide, axis=-1, keepdims=True) + NORM_EPSILON)
    return wide * inverse, inverse


def norm_back(grad, unit, inverse, gain):
    shaped = grad * gain
    inner = jnp.mean(shaped * unit, axis=-1, keepdims=True)
    return inverse * (shaped - unit * inner)


def fold(x, op):
    return op(x.reshape(x.shape[0] // 8, 8, x.shape[1]), axis=0)


def near(table, index):
    last = table.shape[0] - 1
    even = index % 2 == 0
    below = jnp.where(index == 0, 0, table[jnp.maximum(index - 1, 0)])
    above = jnp.where(index == last, 0, table[jnp.minimum(index + 1, last)])
    return table[index], jnp.where(even, above, below), jnp.where(even, below, above)


def attention_kernel(frame_counts, row_counts, query_gain, key_gain, queries, grads, *rest):
    ins, outs, scratch = rest[:8], rest[8:18], rest[18:]
    own_in, te_in, to_in, he_in, ho_in, ce_in, ze_in, zo_in = ins
    own, te, to, he, ho, ce, ze, zo, d_queries, gains = outs
    kn, probs, dps = scratch
    f, fe, fo = near(frame_counts, lax.axis_index("tm"))
    r, re, ro = near(row_counts, lax.axis_index("height"))
    frames = (f, fe, fo, f, f, fe, fe, fo, fo)
    rows = (r, r, r, re, ro, re, ro, re, ro)
    sources = (own_in, te_in, to_in, he_in, ho_in, ce_in.at[0], ce_in.at[1], ze_in, zo_in)
    targets = (own, te, to, he, ho, ce.at[0], ce.at[1], ze, zo)

    q_unit, q_inverse = unit_norm(queries[...])
    gain_q = query_gain[...]
    gain_k = key_gain[...]
    qn = (q_unit * gain_q).astype(jnp.bfloat16)
    gm = jnp.where(
        valid_rows((TILE, HD), f, r), grads[...], jnp.zeros_like(grads[...])
    )
    qt = qn.T
    gt = gm.T

    top = jnp.full((1, TILE), -1e30, jnp.float32)
    total = jnp.zeros((1, TILE), jnp.float32)
    tops = {}
    for j in range(9):
        unit, _ = unit_norm(sources[j][0])
        normed = (unit * gain_k).astype(jnp.bfloat16)
        kn[j] = normed
        bias = jnp.where(valid_rows((TILE, HD), frames[j], rows[j]), 0.0, -1e30)
        tile_top = jnp.full((8, TILE), -1e30, jnp.float32)
        for c in range(0, TILE, CHUNK):
            s = jnp.dot(normed[c : c + CHUNK], qt, preferred_element_type=jnp.float32)
            b = bias[c : c + CHUNK]
            s = s * (SCALE * LOG2E) + jnp.concatenate([b, b, b], axis=1)
            probs[j, c : c + CHUNK] = s
            tile_top = jnp.maximum(tile_top, fold(s, jnp.max))
        new_top = jnp.maximum(top, jnp.max(tile_top, axis=0, keepdims=True))
        part = jnp.zeros((8, TILE), jnp.float32)
        for c in range(0, TILE, CHUNK):
            e = jnp.exp2(probs[j, c : c + CHUNK] - new_top)
            probs[j, c : c + CHUNK] = e
            part = part + fold(e, jnp.sum)
        total = total * jnp.exp2(top - new_top) + jnp.sum(part, axis=0, keepdims=True)
        top = new_top
        tops[j] = new_top

    inverse_total = 1.0 / total
    delta8 = jnp.zeros((8, TILE), jnp.float32)
    for j in range(9):
        factor = jnp.exp2(tops[j] - top) * inverse_total
        v = sources[j][1]
        for c in range(0, TILE, CHUNK):
            dp = jnp.dot(v[c : c + CHUNK], gt, preferred_element_type=jnp.float32)
            p = probs[j, c : c + CHUNK] * factor
            low = p.astype(jnp.bfloat16)
            probs[j, c : c + CHUNK] = p
            dps[j, c : c + CHUNK] = dp
            delta8 = delta8 + fold(low.astype(jnp.float32) * dp, jnp.sum)
            dv = jnp.dot(low, gm, preferred_element_type=jnp.float32).astype(jnp.bfloat16)
            targets[j][1, c : c + CHUNK] = dv
    delta = jnp.sum(delta8, axis=0, keepdims=True)

    dq_t = jnp.zeros((HD, TILE), jnp.float32)
    key_gain_sum = jnp.zeros((8, HD), jnp.float32)
    for j in range(9):
        unit, _ = unit_norm(sources[j][0])
        for c in range(0, TILE, CHUNK):
            ds = (probs[j, c : c + CHUNK] * (dps[j, c : c + CHUNK] - delta) * SCALE).astype(
                jnp.bfloat16
            )
            dk = jnp.dot(ds, qn, preferred_element_type=jnp.float32).astype(jnp.bfloat16)
            targets[j][0, c : c + CHUNK] = dk
            key_gain_sum = key_gain_sum + fold(
                dk.astype(jnp.float32) * unit[c : c + CHUNK], jnp.sum
            )
            dq_t = dq_t + lax.dot_general(
                kn[j, c : c + CHUNK],
                ds,
                (((0,), (0,)), ((), ())),
                preferred_element_type=jnp.float32,
            )
    dq = dq_t.T
    d_queries[...] = norm_back(dq, q_unit, q_inverse, gain_q).astype(jnp.bfloat16)

    @pl.when(pl.program_id(0) == 0)
    def _():
        gains[...] = jnp.zeros_like(gains)

    gains[0:8] += fold(dq * q_unit, jnp.sum)
    gains[8:16] += key_gain_sum


def block_specs():
    row = pl.BlockSpec((TILE, HD), lambda h: (0, h))
    pair = pl.BlockSpec((2, TILE, HD), lambda h: (0, 0, h))
    whole = pl.BlockSpec((1, HD), lambda h: (0, 0))
    return row, pair, whole


def attention(frame_counts, row_counts, query_gain, key_gain, queries, grads, ins):
    heads = queries.shape[1] // HD
    row, pair, whole = block_specs()
    quad = pl.BlockSpec((2, 2, TILE, HD), lambda h: (0, 0, 0, h))
    spec_of = {3: pair, 4: quad}
    low = lambda *lead: jax.ShapeDtypeStruct(lead + queries.shape, jnp.bfloat16)
    return pl.pallas_call(
        attention_kernel,
        grid=(heads,),
        in_specs=[pl.BlockSpec(memory_space=pltpu.SMEM)] * 2
        + [whole, whole, row, row]
        + [spec_of[x.ndim] for x in ins],
        out_specs=[pair] * 5
        + [quad, pair, pair, row, pl.BlockSpec((16, HD), lambda h: (0, 0))],
        out_shape=[low(2)] * 5
        + [low(2, 2), low(2), low(2), low(), jax.ShapeDtypeStruct((16, HD), jnp.float32)],
        scratch_shapes=[
            pltpu.VMEM((9, TILE, HD), jnp.bfloat16),
            pltpu.VMEM((9, TILE, TILE), jnp.float32),
            pltpu.VMEM((9, TILE, TILE), jnp.float32),
        ],
        compiler_params=pltpu.CompilerParams(vmem_limit_bytes=36 * 2**20),
        cost_estimate=pl.CostEstimate(
            flops=heads * 10 * TILE * TILE * 9 * HD,
            bytes_accessed=40 * TILE * queries.shape[1] * 2,
            transcendentals=heads * 9 * TILE * TILE,
        ),
    )(frame_counts, row_counts, query_gain[None], key_gain[None], queries, grads, *ins)


def finish_kernel(key_gain, keys, *rest):
    pairs, (d_keys, d_values) = rest[:-2], rest[-2:]
    dk = jnp.zeros(keys.shape, jnp.float32)
    dv = jnp.zeros(keys.shape, jnp.float32)
    for part in pairs:
        dk = dk + part[0].astype(jnp.float32)
        dv = dv + part[1].astype(jnp.float32)
    unit, inverse = unit_norm(keys[...])
    d_keys[...] = norm_back(dk, unit, inverse, key_gain[...]).astype(jnp.bfloat16)
    d_values[...] = dv.astype(jnp.bfloat16)


def finish(key_gain, keys, pairs):
    heads = keys.shape[1] // HD
    row, pair, whole = block_specs()
    return pl.pallas_call(
        finish_kernel,
        grid=(heads,),
        in_specs=[whole, row] + [pair] * len(pairs),
        out_specs=[row, row],
        out_shape=[jax.ShapeDtypeStruct(keys.shape, jnp.bfloat16)] * 2,
        compiler_params=pltpu.CompilerParams(vmem_limit_bytes=16 * 2**20),
    )(key_gain[None], keys, *pairs)


def swaps(size, first, skip=()):
    route = []
    for i in range(first, size - 1, 2):
        if i not in skip:
            route += [(i, i + 1), (i + 1, i)]
    return route


def total_over(x, axis, bits):
    size = lax.axis_size(axis)
    for bit in bits:
        x = x + lax.ppermute(x, axis, [(i, i ^ bit) for i in range(size)])
    return x


def on_device(
    queries, key_vectors, value_vectors, out_grads, query_gain, key_gain, frame_counts, row_counts
):
    time_count = lax.axis_size("tm")
    height_count = lax.axis_size("height")
    row_count = queries.shape[2]
    feature_count = queries.shape[3]
    keys = key_vectors[0, 0]
    values = value_vectors[0, 0]

    even_t, odd_t = swaps(8, 0), swaps(8, 1, (3,))
    even_h, odd_h = swaps(4, 0), swaps(4, 1)
    key_route = odd_t + [(3, 4), (4, 3)]
    value_route = odd_t + [(3, 0), (4, 7)]
    arrive = [(0, 4), (7, 3)]
    time_index = lax.axis_index("tm")
    across = (time_index == 3) | (time_index == 4)

    tv = lax.ppermute(values, "tm", value_route)
    tk = lax.ppermute(keys, "tm", key_route)
    own = jnp.stack([keys, values])
    he = lax.ppermute(own, "height", even_h)
    ho = lax.ppermute(own, "height", odd_h)
    te = lax.ppermute(own, "tm", even_t)
    vx = lax.ppermute(tv, "tm", arrive)
    he, ho, te, tk = lax.optimization_barrier((he, ho, te, tk))
    ce = lax.ppermute(jnp.stack([he, ho]), "tm", even_t)
    to = jnp.stack([tk, jnp.where(across, vx, tv)])
    ze = lax.ppermute(to, "height", even_h)
    zo = lax.ppermute(to, "height", odd_h)

    outs = attention(
        frame_counts,
        row_counts,
        query_gain,
        key_gain,
        queries[0, 0],
        out_grads[0, 0],
        [own, te, to, he, ho, ce, ze, zo],
    )
    own, te, to, he, ho, ce, ze, zo, d_queries, gain_parts = outs

    def add(*parts):
        return sum(x.astype(jnp.float32) for x in parts).astype(jnp.bfloat16)

    ze = lax.ppermute(ze, "height", even_h)
    zo = lax.ppermute(zo, "height", odd_h)
    ce = lax.ppermute(ce, "tm", even_t)
    gain_local = jnp.sum(gain_parts.reshape(2, 8, HD), axis=1)
    gain_local = total_over(gain_local, "dp", (1, 2, 4))
    gain_local, ze, zo = lax.optimization_barrier((gain_local, ze, zo))
    to = add(to, ze, zo)
    gain_local, _ = lax.optimization_barrier((gain_local, to))
    to = lax.ppermute(to, "tm", key_route)
    he = lax.ppermute(add(he, ce[0]), "height", even_h)
    ho = lax.ppermute(add(ho, ce[1]), "height", odd_h)
    gain_local, te = lax.optimization_barrier((total_over(gain_local, "tm", (1, 2)), te))
    te = lax.ppermute(te, "tm", even_t)
    inner = [t for t in range(8) if t % 4 in (1, 2)]
    x = gain_local
    x = x + lax.ppermute(x, "tm", [(t, t ^ 4) for t in inner])
    for bit in (1, 2):
        route = [(4 * t + h, 4 * t + (h ^ bit)) for t in inner for h in range(4)]
        x = x + lax.ppermute(x, ("tm", "height"), route)
    outer = lax.ppermute(x, "tm", [(1, 0), (2, 3), (5, 4), (6, 7)])
    place = lax.rem(lax.axis_index("tm"), 4)
    gain_total = jnp.where((place == 1) | (place == 2), x, outer)
    d_keys, d_values = finish(key_gain, keys, [own, te, to, he, ho])

    head_total = lax.axis_size("dp") * (feature_count // HD)
    scaling = 1.0 / math.sqrt(time_count * height_count * row_count * head_total)
    gain_grads = gain_total * scaling
    return (d_queries[None, None], d_keys[None, None], d_values[None, None], gain_grads)


def solution(mesh):
    split = P("tm", "height", None, "dp")
    return jax.shard_map(
        on_device,
        mesh=mesh,
        in_specs=(split,) * 4 + (P(),) * 4,
        out_specs=(split,) * 3 + (P(),),
        check_vma=False,
    )
```

```python
import functools
import math

import jax
import jax.numpy as jnp
from jax import lax
from jax.experimental import pallas as pl
from jax.experimental.pallas import tpu as pltpu
from jax.sharding import PartitionSpec as P

HD = 128
TF = 6
TH = 8
TW = 8
TILE = TF * TH * TW
NORM_EPSILON = 1e-06
SCALE = 1.0 / math.sqrt(HD)
LOG2E = math.log2(math.e)
CHUNK = 384


def valid_rows(shape, frame_limit, row_limit):
    token = lax.broadcasted_iota(jnp.int32, shape, 0)
    return ((token >> 6) < frame_limit) & (((token >> 3) & 7) < row_limit)


def unit_norm(raw):
    wide = raw.astype(jnp.float32)
    inverse = lax.rsqrt(jnp.mean(wide * wide, axis=-1, keepdims=True) + NORM_EPSILON)
    return wide * inverse, inverse


def norm_back(grad, unit, inverse, gain):
    shaped = grad * gain
    inner = jnp.mean(shaped * unit, axis=-1, keepdims=True)
    return inverse * (shaped - unit * inner)


def fold(x, op):
    return op(x.reshape(x.shape[0] // 8, 8, x.shape[1]), axis=0)


def near(table, index):
    last = table.shape[0] - 1
    even = index % 2 == 0
    below = jnp.where(index == 0, 0, table[jnp.maximum(index - 1, 0)])
    above = jnp.where(index == last, 0, table[jnp.minimum(index + 1, last)])
    return table[index], jnp.where(even, above, below), jnp.where(even, below, above)


def attention_kernel(frame_counts, row_counts, query_gain, key_gain, queries, grads, *rest):
    sources, targets, rest = rest[:9], rest[9:18], rest[18:]
    d_queries, gains, kn, probs, dps = rest
    f, fe, fo = near(frame_counts, lax.axis_index("tm"))
    r, re, ro = near(row_counts, lax.axis_index("height"))
    frames = (f, fe, fo, f, f, fe, fe, fo, fo)
    rows = (r, r, r, re, ro, re, ro, re, ro)

    q_unit, q_inverse = unit_norm(queries[...])
    gain_q = query_gain[...]
    gain_k = key_gain[...]
    qn = (q_unit * gain_q).astype(jnp.bfloat16)
    gm = jnp.where(
        valid_rows((TILE, HD), f, r), grads[...], jnp.zeros_like(grads[...])
    )
    qt = qn.T
    gt = gm.T

    top = jnp.full((1, TILE), -1e30, jnp.float32)
    total = jnp.zeros((1, TILE), jnp.float32)
    tops = {}
    for j in range(9):
        unit, _ = unit_norm(sources[j][0])
        normed = (unit * gain_k).astype(jnp.bfloat16)
        kn[j] = normed
        bias = jnp.where(valid_rows((TILE, HD), frames[j], rows[j]), 0.0, -1e30)
        tile_top = jnp.full((8, TILE), -1e30, jnp.float32)
        for c in range(0, TILE, CHUNK):
            s = jnp.dot(normed[c : c + CHUNK], qt, preferred_element_type=jnp.float32)
            b = bias[c : c + CHUNK]
            s = s * (SCALE * LOG2E) + jnp.concatenate([b, b, b], axis=1)
            probs[j, c : c + CHUNK] = s
            tile_top = jnp.maximum(tile_top, fold(s, jnp.max))
        new_top = jnp.maximum(top, jnp.max(tile_top, axis=0, keepdims=True))
        part = jnp.zeros((8, TILE), jnp.float32)
        for c in range(0, TILE, CHUNK):
            e = jnp.exp2(probs[j, c : c + CHUNK] - new_top)
            probs[j, c : c + CHUNK] = e
            part = part + fold(e, jnp.sum)
        total = total * jnp.exp2(top - new_top) + jnp.sum(part, axis=0, keepdims=True)
        top = new_top
        tops[j] = new_top

    inverse_total = 1.0 / total
    delta8 = jnp.zeros((8, TILE), jnp.float32)
    for j in range(9):
        factor = jnp.exp2(tops[j] - top) * inverse_total
        v = sources[j][1]
        for c in range(0, TILE, CHUNK):
            dp = jnp.dot(v[c : c + CHUNK], gt, preferred_element_type=jnp.float32)
            p = probs[j, c : c + CHUNK] * factor
            low = p.astype(jnp.bfloat16)
            probs[j, c : c + CHUNK] = p
            dps[j, c : c + CHUNK] = dp
            delta8 = delta8 + fold(low.astype(jnp.float32) * dp, jnp.sum)
            dv = jnp.dot(low, gm, preferred_element_type=jnp.float32).astype(jnp.bfloat16)
            targets[j][1, c : c + CHUNK] = dv
    delta = jnp.sum(delta8, axis=0, keepdims=True)

    dq_t = jnp.zeros((HD, TILE), jnp.float32)
    key_gain_sum = jnp.zeros((8, HD), jnp.float32)
    for j in range(9):
        unit, _ = unit_norm(sources[j][0])
        for c in range(0, TILE, CHUNK):
            ds = (probs[j, c : c + CHUNK] * (dps[j, c : c + CHUNK] - delta) * SCALE).astype(
                jnp.bfloat16
            )
            dk = jnp.dot(ds, qn, preferred_element_type=jnp.float32).astype(jnp.bfloat16)
            targets[j][0, c : c + CHUNK] = dk
            key_gain_sum = key_gain_sum + fold(
                dk.astype(jnp.float32) * unit[c : c + CHUNK], jnp.sum
            )
            dq_t = dq_t + lax.dot_general(
                kn[j, c : c + CHUNK],
                ds,
                (((0,), (0,)), ((), ())),
                preferred_element_type=jnp.float32,
            )
    dq = dq_t.T
    d_queries[...] = norm_back(dq, q_unit, q_inverse, gain_q).astype(jnp.bfloat16)

    @pl.when(pl.program_id(0) == 0)
    def _():
        gains[...] = jnp.zeros_like(gains)

    gains[0:8] += fold(dq * q_unit, jnp.sum)
    gains[8:16] += key_gain_sum


def block_specs():
    row = pl.BlockSpec((TILE, HD), lambda h: (0, h))
    pair = pl.BlockSpec((2, TILE, HD), lambda h: (0, 0, h))
    whole = pl.BlockSpec((1, HD), lambda h: (0, 0))
    return row, pair, whole


def attention(frame_counts, row_counts, query_gain, key_gain, queries, grads, ins):
    heads = queries.shape[1] // HD
    row, pair, whole = block_specs()
    low = lambda *lead: jax.ShapeDtypeStruct(lead + queries.shape, jnp.bfloat16)
    return pl.pallas_call(
        attention_kernel,
        grid=(heads,),
        in_specs=[pl.BlockSpec(memory_space=pltpu.SMEM)] * 2
        + [whole, whole, row, row]
        + [pair] * 9,
        out_specs=[pair] * 9 + [row, pl.BlockSpec((16, HD), lambda h: (0, 0))],
        out_shape=[low(2)] * 9 + [low(), jax.ShapeDtypeStruct((16, HD), jnp.float32)],
        scratch_shapes=[
            pltpu.VMEM((9, TILE, HD), jnp.bfloat16),
            pltpu.VMEM((9, TILE, TILE), jnp.float32),
            pltpu.VMEM((9, TILE, TILE), jnp.float32),
        ],
        compiler_params=pltpu.CompilerParams(vmem_limit_bytes=36 * 2**20),
        cost_estimate=pl.CostEstimate(
            flops=heads * 10 * TILE * TILE * 9 * HD,
            bytes_accessed=40 * TILE * queries.shape[1] * 2,
            transcendentals=heads * 9 * TILE * TILE,
        ),
    )(frame_counts, row_counts, query_gain[None], key_gain[None], queries, grads, *ins)


def finish_kernel(key_gain, keys, *rest):
    pairs, (d_keys, d_values) = rest[:-2], rest[-2:]
    dk = jnp.zeros(keys.shape, jnp.float32)
    dv = jnp.zeros(keys.shape, jnp.float32)
    for part in pairs:
        dk = dk + part[0].astype(jnp.float32)
        dv = dv + part[1].astype(jnp.float32)
    unit, inverse = unit_norm(keys[...])
    d_keys[...] = norm_back(dk, unit, inverse, key_gain[...]).astype(jnp.bfloat16)
    d_values[...] = dv.astype(jnp.bfloat16)


def finish(key_gain, keys, pairs):
    heads = keys.shape[1] // HD
    row, pair, whole = block_specs()
    return pl.pallas_call(
        finish_kernel,
        grid=(heads,),
        in_specs=[whole, row] + [pair] * len(pairs),
        out_specs=[row, row],
        out_shape=[jax.ShapeDtypeStruct(keys.shape, jnp.bfloat16)] * 2,
        compiler_params=pltpu.CompilerParams(vmem_limit_bytes=16 * 2**20),
    )(key_gain[None], keys, *pairs)


def swaps(size, first, skip=()):
    route = []
    for i in range(first, size - 1, 2):
        if i not in skip:
            route += [(i, i + 1), (i + 1, i)]
    return route


def total_over(x, axis, bits):
    size = lax.axis_size(axis)
    for bit in bits:
        x = x + lax.ppermute(x, axis, [(i, i ^ bit) for i in range(size)])
    return x


def on_device(
    queries, key_vectors, value_vectors, out_grads, query_gain, key_gain, frame_counts, row_counts
):
    time_count = lax.axis_size("tm")
    height_count = lax.axis_size("height")
    row_count = queries.shape[2]
    feature_count = queries.shape[3]
    keys = key_vectors[0, 0]
    values = value_vectors[0, 0]

    even_t, odd_t = swaps(8, 0), swaps(8, 1, (3,))
    even_h, odd_h = swaps(4, 0), swaps(4, 1)
    key_route = odd_t + [(3, 4), (4, 3)]
    value_route = odd_t + [(3, 0), (4, 7)]
    arrive = [(0, 4), (7, 3)]
    time_index = lax.axis_index("tm")
    across = (time_index == 3) | (time_index == 4)

    tv = lax.ppermute(values, "tm", value_route)
    tk = lax.ppermute(keys, "tm", key_route)
    own = jnp.stack([keys, values])
    he = lax.ppermute(own, "height", even_h)
    ho = lax.ppermute(own, "height", odd_h)
    te = lax.ppermute(own, "tm", even_t)
    vx = lax.ppermute(tv, "tm", arrive)
    he, ho, te = lax.optimization_barrier((he, ho, te))
    ce = lax.ppermute(he, "tm", even_t)
    co = lax.ppermute(ho, "tm", even_t)
    to = jnp.stack([tk, jnp.where(across, vx, tv)])
    ze = lax.ppermute(to, "height", even_h)
    zo = lax.ppermute(to, "height", odd_h)

    outs = attention(
        frame_counts,
        row_counts,
        query_gain,
        key_gain,
        queries[0, 0],
        out_grads[0, 0],
        [own, te, to, he, ho, ce, co, ze, zo],
    )
    own, te, to, he, ho, ce, co, ze, zo, d_queries, gain_parts = outs

    def add(*parts):
        return sum(x.astype(jnp.float32) for x in parts).astype(jnp.bfloat16)

    ze = lax.ppermute(ze, "height", even_h)
    zo = lax.ppermute(zo, "height", odd_h)
    ce = lax.ppermute(ce, "tm", even_t)
    co = lax.ppermute(co, "tm", even_t)
    gain_local = jnp.sum(gain_parts.reshape(2, 8, HD), axis=1)
    gain_local = total_over(gain_local, "dp", (1, 2, 4))
    gain_local, ze, zo = lax.optimization_barrier((gain_local, ze, zo))
    to = add(to, ze, zo)
    gain_local, _ = lax.optimization_barrier((gain_local, to))
    to = lax.ppermute(to, "tm", key_route)
    he = lax.ppermute(add(he, ce), "height", even_h)
    ho = lax.ppermute(add(ho, co), "height", odd_h)
    gain_local, te = lax.optimization_barrier((total_over(gain_local, "tm", (1, 2)), te))
    te = lax.ppermute(te, "tm", even_t)
    inner = [t for t in range(8) if t % 4 in (1, 2)]
    x = gain_local
    x = x + lax.ppermute(x, "tm", [(t, t ^ 4) for t in inner])
    for bit in (1, 2):
        route = [(4 * t + h, 4 * t + (h ^ bit)) for t in inner for h in range(4)]
        x = x + lax.ppermute(x, ("tm", "height"), route)
    outer = lax.ppermute(x, "tm", [(1, 0), (2, 3), (5, 4), (6, 7)])
    place = lax.rem(lax.axis_index("tm"), 4)
    gain_total = jnp.where((place == 1) | (place == 2), x, outer)
    d_keys, d_values = finish(key_gain, keys, [own, te, to, he, ho])

    head_total = lax.axis_size("dp") * (feature_count // HD)
    scaling = 1.0 / math.sqrt(time_count * height_count * row_count * head_total)
    gain_grads = gain_total * scaling
    return (d_queries[None, None], d_keys[None, None], d_values[None, None], gain_grads)


def solution(mesh):
    split = P("tm", "height", None, "dp")
    return jax.shard_map(
        on_device,
        mesh=mesh,
        in_specs=(split,) * 4 + (P(),) * 4,
        out_specs=(split,) * 3 + (P(),),
        check_vma=False,
    )
```

```python
import functools
import math

import jax
import jax.numpy as jnp
from jax import lax
from jax.experimental import pallas as pl
from jax.experimental.pallas import tpu as pltpu
from jax.sharding import PartitionSpec as P

HD = 128
TF = 6
TH = 8
TW = 8
TILE = TF * TH * TW
NORM_EPSILON = 1e-06
SCALE = 1.0 / math.sqrt(HD)
LOG2E = math.log2(math.e)
TAIL = 1024
ROOM = 9 * TILE + TAIL
GROUPS = {HD: 9, 2 * HD: 6, 3 * HD: 3}


def below(shape, count):
    return lax.broadcasted_iota(jnp.int32, shape, 0) < count


def pack_rows(held, block, rows):
    held[...] = jnp.zeros_like(held)
    for frame in range(TF):
        first = pl.multiple_of(frame * rows * TW, TW)
        held[pl.ds(first, TH * TW)] = block[frame * TH * TW : (frame + 1) * TH * TW]


def unpack_rows(out, held, frames, rows):
    for frame in range(TF):
        first = pl.multiple_of(frame * rows * TW, TW)
        block = held[pl.ds(first, TH * TW)]
        keep = below(block.shape, jnp.where(frame < frames, rows * TW, 0))
        out[frame * TH * TW : (frame + 1) * TH * TW] = jnp.where(keep, block, 0.0).astype(out.dtype)


def unit_norm(raw):
    wide = raw.astype(jnp.float32)
    inverse = lax.rsqrt(jnp.mean(wide * wide, axis=-1, keepdims=True) + NORM_EPSILON)
    return wide * inverse, inverse


def norm_back(grad, unit, inverse, gain):
    shaped = grad * gain
    inner = jnp.mean(shaped * unit, axis=-1, keepdims=True)
    return inverse * (shaped - unit * inner)


def fold(x, op):
    return op(x.reshape(x.shape[0] // 8, 8, x.shape[1]), axis=0)


def near(table, index):
    last = table.shape[0] - 1
    even = index % 2 == 0
    below = jnp.where(index == 0, 0, table[jnp.maximum(index - 1, 0)])
    above = jnp.where(index == last, 0, table[jnp.minimum(index + 1, last)])
    return table[index], jnp.where(even, above, below), jnp.where(even, below, above)


def attention_kernel(frame_counts, row_counts, query_gain, key_gain, queries, grads, *rest):
    for head in range(queries.shape[-1] // HD):
        part = pl.ds(head * HD, HD)
        cut = [x.at[..., part] for x in rest[:19]]
        one_head(
            head, frame_counts, row_counts, query_gain, key_gain,
            queries.at[:, part], grads.at[:, part], *cut, *rest[19:],
        )


def one_head(
    head, frame_counts, row_counts, query_gain, key_gain, queries, grads, *rest
):
    sources, targets, rest = rest[:9], rest[9:18], rest[18:]
    d_queries, gains, kn, vs, bias, units, grads_kv, probs, dps, wide = rest
    f, fe, fo = near(frame_counts, lax.axis_index("tm"))
    r, re, ro = near(row_counts, lax.axis_index("height"))
    frames = (f, fe, fo, f, f, fe, fe, fo, fo)
    rows = (r, r, r, re, ro, re, ro, re, ro)
    counts = [x * y * TW for x, y in zip(frames, rows)]

    q_unit, q_inverse = unit_norm(queries[...])
    gain_q = query_gain[...]
    gain_k = key_gain[...]
    qn = (q_unit * gain_q).astype(jnp.bfloat16)
    low_grads = grads[...]
    gm = jnp.where(below((TILE, HD), counts[0]), low_grads, jnp.zeros_like(low_grads))

    starts = [jnp.int32(0)]
    for j in range(9):
        at = pl.ds(pl.multiple_of(starts[j], HD), TILE)
        unit, _ = unit_norm(sources[j][0])
        units[at] = unit
        kn[at] = (unit * gain_k).astype(jnp.bfloat16)
        vs[at] = sources[j][1]
        bias[at] = jnp.where(below((TILE, HD), counts[j]), 0.0, -1e30)
        starts.append(starts[j] + ((counts[j] + HD - 1) >> 7) * HD)
    at = pl.ds(pl.multiple_of(starts[9], HD), TAIL)
    kn[at] = jnp.zeros((TAIL, HD), jnp.bfloat16)
    vs[at] = jnp.zeros((TAIL, HD), jnp.bfloat16)
    bias[at] = jnp.full((TAIL, HD), -1e30, jnp.float32)
    used = starts[9] >> 7
    wide[...] = jnp.zeros_like(wide)

    def attend(width):
        qs, gs = qn[:width], gm[:width]
        qt, gt = qs.T, gs.T
        size = GROUPS[width]
        groups = lax.div(used + (size - 1), jnp.int32(size))

        def rows_of(i):
            return pl.ds(pl.multiple_of(i * (size * HD), HD), size * HD)

        def score(i, top):
            s = jnp.dot(kn[rows_of(i)], qt, preferred_element_type=jnp.float32)
            b = bias[rows_of(i)]
            s = s * (SCALE * LOG2E) + jnp.concatenate([b] * (width // HD), axis=1)
            probs[rows_of(i), :width] = s
            return jnp.maximum(top, fold(s, jnp.max))

        top = lax.fori_loop(0, groups, score, jnp.full((8, width), -1e30, jnp.float32))
        top = jnp.max(top, axis=0, keepdims=True)

        def power(i, total):
            e = jnp.exp2(probs[rows_of(i), :width] - top)
            probs[rows_of(i), :width] = e
            return total + fold(e, jnp.sum)

        total = lax.fori_loop(0, groups, power, jnp.zeros((8, width), jnp.float32))
        inverse = 1.0 / jnp.sum(total, axis=0, keepdims=True)

        def weigh(i, delta):
            dp = jnp.dot(vs[rows_of(i)], gt, preferred_element_type=jnp.float32)
            p = probs[rows_of(i), :width] * inverse
            low = p.astype(jnp.bfloat16)
            probs[rows_of(i), :width] = p
            dps[rows_of(i), :width] = dp
            dv = jnp.dot(low, gs, preferred_element_type=jnp.float32)
            grads_kv[1, rows_of(i)] = dv.astype(jnp.bfloat16)
            return delta + fold(low.astype(jnp.float32) * dp, jnp.sum)

        delta = lax.fori_loop(0, groups, weigh, jnp.zeros((8, width), jnp.float32))
        delta = jnp.sum(delta, axis=0, keepdims=True)

        def back(i, dq_t):
            ds = probs[rows_of(i), :width] * (dps[rows_of(i), :width] - delta) * SCALE
            ds = ds.astype(jnp.bfloat16)
            dk = jnp.dot(ds, qs, preferred_element_type=jnp.float32)
            grads_kv[0, rows_of(i)] = dk.astype(jnp.bfloat16)
            return dq_t + lax.dot_general(
                kn[rows_of(i)], ds, (((0,), (0,)), ((), ())), preferred_element_type=jnp.float32
            )

        dq_t = lax.fori_loop(0, groups, back, jnp.zeros((HD, width), jnp.float32))
        wide[:width] = dq_t.T

    for width in (HD, 2 * HD, 3 * HD):
        pl.when((counts[0] > width - HD) & (counts[0] <= width))(functools.partial(attend, width))

    key_gain_sum = jnp.zeros((8, HD), jnp.float32)
    for j in range(9):
        at = pl.ds(pl.multiple_of(starts[j], HD), TILE)
        keep = below((TILE, HD), counts[j])
        zero = jnp.zeros((TILE, HD), jnp.bfloat16)
        dk = jnp.where(keep, grads_kv[0, at], zero)
        targets[j][0] = dk
        targets[j][1] = jnp.where(keep, grads_kv[1, at], zero)
        key_gain_sum = key_gain_sum + fold(dk.astype(jnp.float32) * units[at], jnp.sum)

    dq = wide[...]
    query_gain_sum = fold(dq * q_unit, jnp.sum)
    wide[...] = norm_back(dq, q_unit, q_inverse, gain_q)
    unpack_rows(d_queries, wide, f, r)

    if head == 0:
        gains[...] = jnp.zeros_like(gains)

    gains[0:8] += query_gain_sum
    gains[8:16] += key_gain_sum


def pack_kernel(row_counts, *refs):
    ins, (own, *outs, held) = refs[:4], refs[4:]
    rows = row_counts[lax.axis_index("height")]
    for i, (block, out) in enumerate(zip(ins, outs)):
        pack_rows(held, block[...].astype(jnp.float32), rows)
        packed = held[...].astype(out.dtype)
        out[...] = packed
        if i < 2:
            own[i] = packed


def pack(row_counts, *arrays):
    shape = arrays[0].shape
    heads = shape[1] // HD
    row, pair, _ = block_specs()
    return pl.pallas_call(
        pack_kernel,
        grid=(heads,),
        in_specs=[pl.BlockSpec(memory_space=pltpu.SMEM)] + [row] * 4,
        out_specs=[pair] + [row] * 4,
        out_shape=[jax.ShapeDtypeStruct((2,) + shape, jnp.bfloat16)]
        + [jax.ShapeDtypeStruct(shape, jnp.bfloat16)] * 4,
        scratch_shapes=[pltpu.VMEM((TILE, HD), jnp.float32)],
        compiler_params=pltpu.CompilerParams(vmem_limit_bytes=56 * 2**20),
    )(row_counts, *arrays)


def block_specs():
    row = pl.BlockSpec((TILE, HD), lambda h: (0, h))
    pair = pl.BlockSpec((2, TILE, HD), lambda h: (0, 0, h))
    whole = pl.BlockSpec((1, HD), lambda h: (0, 0))
    return row, pair, whole


def attention(frame_counts, row_counts, query_gain, key_gain, queries, grads, ins):
    heads = queries.shape[1] // HD
    row, pair, whole = block_specs()
    low = lambda *lead: jax.ShapeDtypeStruct(lead + queries.shape, jnp.bfloat16)
    return pl.pallas_call(
        attention_kernel,
        in_specs=[pl.BlockSpec(memory_space=pltpu.SMEM)] * 2
        + [pl.BlockSpec(memory_space=pltpu.VMEM)] * 13,
        out_specs=[pl.BlockSpec(memory_space=pltpu.VMEM)] * 11,
        out_shape=[low(2)] * 9 + [low(), jax.ShapeDtypeStruct((16, HD), jnp.float32)],
        scratch_shapes=[
            pltpu.VMEM((ROOM, HD), jnp.bfloat16),
            pltpu.VMEM((ROOM, HD), jnp.bfloat16),
            pltpu.VMEM((ROOM, HD), jnp.float32),
            pltpu.VMEM((ROOM, HD), jnp.float32),
            pltpu.VMEM((2, ROOM, HD), jnp.bfloat16),
            pltpu.VMEM((ROOM, TILE), jnp.float32),
            pltpu.VMEM((ROOM, TILE), jnp.float32),
            pltpu.VMEM((TILE, HD), jnp.float32),
        ],
        compiler_params=pltpu.CompilerParams(vmem_limit_bytes=44 * 2**20),
        cost_estimate=pl.CostEstimate(
            flops=heads * 10 * TILE * TILE * 9 * HD,
            bytes_accessed=40 * TILE * queries.shape[1] * 2,
            transcendentals=heads * 9 * TILE * TILE,
        ),
    )(frame_counts, row_counts, query_gain[None], key_gain[None], queries, grads, *ins)


def finish_kernel(frame_counts, row_counts, key_gain, keys, *rest):
    pairs, (d_keys, d_values, held) = rest[:-3], rest[-3:]
    time_index = lax.axis_index("tm")
    dk = jnp.zeros(keys.shape, jnp.float32)
    dv = jnp.zeros(keys.shape, jnp.float32)
    for part in pairs:
        dk = dk + part[0].astype(jnp.float32)
        dv = dv + part[1].astype(jnp.float32)
    unit, inverse = unit_norm(keys[...])
    frames, rows = frame_counts[time_index], row_counts[lax.axis_index("height")]
    held[...] = norm_back(dk, unit, inverse, key_gain[...])
    unpack_rows(d_keys, held, frames, rows)
    held[...] = dv
    unpack_rows(d_values, held, frames, rows)


def finish(frame_counts, row_counts, key_gain, keys, pairs):
    heads = keys.shape[1] // HD
    row, pair, whole = block_specs()
    return pl.pallas_call(
        finish_kernel,
        grid=(heads,),
        in_specs=[pl.BlockSpec(memory_space=pltpu.SMEM)] * 2
        + [whole, row]
        + [pair] * len(pairs),
        out_specs=[row, row],
        out_shape=[jax.ShapeDtypeStruct(keys.shape, jnp.bfloat16)] * 2,
        scratch_shapes=[pltpu.VMEM((TILE, HD), jnp.float32)],
        compiler_params=pltpu.CompilerParams(vmem_limit_bytes=16 * 2**20),
    )(frame_counts, row_counts, key_gain[None], keys, *pairs)


def swaps(size, first, skip=()):
    route = []
    for i in range(first, size - 1, 2):
        if i not in skip:
            route += [(i, i + 1), (i + 1, i)]
    return route


def total_over(x, axis, bits):
    size = lax.axis_size(axis)
    for bit in bits:
        x = x + lax.ppermute(x, axis, [(i, i ^ bit) for i in range(size)])
    return x


def on_device(
    queries, key_vectors, value_vectors, out_grads, query_gain, key_gain, frame_counts, row_counts
):
    time_count = lax.axis_size("tm")
    height_count = lax.axis_size("height")
    row_count = queries.shape[2]
    feature_count = queries.shape[3]
    own, keys, values, packed_queries, grads = pack(
        row_counts, key_vectors[0, 0], value_vectors[0, 0], queries[0, 0], out_grads[0, 0]
    )

    even_t, odd_t = swaps(8, 0), swaps(8, 1, (3,))
    even_h, odd_h = swaps(4, 0), swaps(4, 1)
    key_route = odd_t + [(3, 4), (4, 3)]
    value_route = odd_t + [(3, 0), (4, 7)]
    arrive = [(0, 4), (7, 3)]
    time_index = lax.axis_index("tm")
    across = (time_index == 3) | (time_index == 4)

    tv = lax.ppermute(values, "tm", value_route)
    tk = lax.ppermute(keys, "tm", key_route)
    he = lax.ppermute(own, "height", even_h)
    ho = lax.ppermute(own, "height", odd_h)
    te = lax.ppermute(own, "tm", even_t)
    vx = lax.ppermute(tv, "tm", arrive)
    he, ho, te = lax.optimization_barrier((he, ho, te))
    ce = lax.ppermute(he, "tm", even_t)
    co = lax.ppermute(ho, "tm", even_t)
    to = jnp.stack([tk, jnp.where(across, vx, tv)])
    ze = lax.ppermute(to, "height", even_h)
    zo = lax.ppermute(to, "height", odd_h)

    outs = attention(
        frame_counts,
        row_counts,
        query_gain,
        key_gain,
        packed_queries,
        grads,
        [own, te, to, he, ho, ce, co, ze, zo],
    )
    own, te, to, he, ho, ce, co, ze, zo, d_queries, gain_parts = outs

    def add(*parts):
        return sum(x.astype(jnp.float32) for x in parts).astype(jnp.bfloat16)

    ze = lax.ppermute(ze, "height", even_h)
    zo = lax.ppermute(zo, "height", odd_h)
    ce = lax.ppermute(ce, "tm", even_t)
    co = lax.ppermute(co, "tm", even_t)
    gain_local = jnp.sum(gain_parts.reshape(2, 8, HD), axis=1)
    gain_local = total_over(total_over(gain_local, "tm", (3,)), "dp", (1, 2))
    gain_local, ze, zo = lax.optimization_barrier((gain_local, ze, zo))
    to = add(to, ze, zo)
    gain_local, _ = lax.optimization_barrier((gain_local, to))
    to = lax.ppermute(to, "tm", key_route)
    he = lax.ppermute(add(he, ce), "height", even_h)
    ho = lax.ppermute(add(ho, co), "height", odd_h)
    gain_local = total_over(total_over(gain_local, "dp", (4,)), "tm", (1,))
    gain_local, te = lax.optimization_barrier((gain_local, te))
    te = lax.ppermute(te, "tm", even_t)
    inner = [t for t in range(8) if t % 4 in (1, 2)]
    x = gain_local
    x = x + lax.ppermute(x, "tm", [(t, t ^ 4) for t in inner])
    for bit in (1, 2):
        route = [(4 * t + h, 4 * t + (h ^ bit)) for t in inner for h in range(4)]
        x = x + lax.ppermute(x, ("tm", "height"), route)
    outer = lax.ppermute(x, "tm", [(1, 0), (2, 3), (5, 4), (6, 7)])
    place = lax.rem(lax.axis_index("tm"), 4)
    gain_total = jnp.where((place == 1) | (place == 2), x, outer)
    d_keys, d_values = finish(frame_counts, row_counts, key_gain, keys, [own, te, to, he, ho])

    head_total = lax.axis_size("dp") * (feature_count // HD)
    scaling = 1.0 / math.sqrt(time_count * height_count * row_count * head_total)
    gain_grads = gain_total * scaling
    return (d_queries[None, None], d_keys[None, None], d_values[None, None], gain_grads)


def solution(mesh):
    split = P("tm", "height", None, "dp")
    return jax.shard_map(
        on_device,
        mesh=mesh,
        in_specs=(split,) * 4 + (P(),) * 4,
        out_specs=(split,) * 3 + (P(),),
        check_vma=False,
    )
```

```python
import functools
import math

import jax
import jax.numpy as jnp
from jax import lax
from jax.experimental import pallas as pl
from jax.experimental.pallas import tpu as pltpu
from jax.sharding import PartitionSpec as P

HD = 128
TF = 6
TH = 8
TW = 8
TILE = TF * TH * TW
NORM_EPSILON = 1e-06
SCALE = 1.0 / math.sqrt(HD)
LOG2E = math.log2(math.e)
CHUNK = 384


def valid_rows(shape, frame_limit, row_limit):
    token = lax.broadcasted_iota(jnp.int32, shape, 0)
    return ((token >> 6) < frame_limit) & (((token >> 3) & 7) < row_limit)


def unit_norm(raw):
    wide = raw.astype(jnp.float32)
    inverse = lax.rsqrt(jnp.mean(wide * wide, axis=-1, keepdims=True) + NORM_EPSILON)
    return wide * inverse, inverse


def norm_back(grad, unit, inverse, gain):
    shaped = grad * gain
    inner = jnp.mean(shaped * unit, axis=-1, keepdims=True)
    return inverse * (shaped - unit * inner)


def fold(x, op):
    return op(x.reshape(x.shape[0] // 8, 8, x.shape[1]), axis=0)


def near(table, index):
    last = table.shape[0] - 1
    even = index % 2 == 0
    below = jnp.where(index == 0, 0, table[jnp.maximum(index - 1, 0)])
    above = jnp.where(index == last, 0, table[jnp.minimum(index + 1, last)])
    return table[index], jnp.where(even, above, below), jnp.where(even, below, above)


def attention_kernel(frame_counts, row_counts, query_gain, key_gain, queries, grads, *rest):
    for head in range(queries.shape[-1] // HD):
        part = pl.ds(head * HD, HD)
        cut = [x.at[..., part] for x in rest[:19]]
        one_head(
            head, frame_counts, row_counts, query_gain, key_gain,
            queries.at[:, part], grads.at[:, part], *cut, *rest[19:],
        )


def one_head(
    head, frame_counts, row_counts, query_gain, key_gain, queries, grads, *rest
):
    sources, targets, rest = rest[:9], rest[9:18], rest[18:]
    d_queries, gains, kn, probs, dps = rest
    f, fe, fo = near(frame_counts, lax.axis_index("tm"))
    r, re, ro = near(row_counts, lax.axis_index("height"))
    frames = (f, fe, fo, f, f, fe, fe, fo, fo)
    rows = (r, r, r, re, ro, re, ro, re, ro)

    q_unit, q_inverse = unit_norm(queries[...])
    gain_q = query_gain[...]
    gain_k = key_gain[...]
    qn = (q_unit * gain_q).astype(jnp.bfloat16)
    gm = jnp.where(
        valid_rows((TILE, HD), f, r), grads[...], jnp.zeros_like(grads[...])
    )
    qt = qn.T
    gt = gm.T

    top = jnp.full((1, TILE), -1e30, jnp.float32)
    total = jnp.zeros((1, TILE), jnp.float32)
    tops = {}
    for j in range(9):
        unit, _ = unit_norm(sources[j][0])
        normed = (unit * gain_k).astype(jnp.bfloat16)
        kn[j] = normed
        bias = jnp.where(valid_rows((TILE, HD), frames[j], rows[j]), 0.0, -1e30)
        tile_top = jnp.full((8, TILE), -1e30, jnp.float32)
        for c in range(0, TILE, CHUNK):
            s = jnp.dot(normed[c : c + CHUNK], qt, preferred_element_type=jnp.float32)
            b = bias[c : c + CHUNK]
            s = s * (SCALE * LOG2E) + jnp.concatenate([b, b, b], axis=1)
            probs[j, c : c + CHUNK] = s
            tile_top = jnp.maximum(tile_top, fold(s, jnp.max))
        new_top = jnp.maximum(top, jnp.max(tile_top, axis=0, keepdims=True))
        part = jnp.zeros((8, TILE), jnp.float32)
        for c in range(0, TILE, CHUNK):
            e = jnp.exp2(probs[j, c : c + CHUNK] - new_top)
            probs[j, c : c + CHUNK] = e
            part = part + fold(e, jnp.sum)
        total = total * jnp.exp2(top - new_top) + jnp.sum(part, axis=0, keepdims=True)
        top = new_top
        tops[j] = new_top

    inverse_total = 1.0 / total
    delta8 = jnp.zeros((8, TILE), jnp.float32)
    for j in range(9):
        factor = jnp.exp2(tops[j] - top) * inverse_total
        v = sources[j][1]
        for c in range(0, TILE, CHUNK):
            dp = jnp.dot(v[c : c + CHUNK], gt, preferred_element_type=jnp.float32)
            p = probs[j, c : c + CHUNK] * factor
            low = p.astype(jnp.bfloat16)
            probs[j, c : c + CHUNK] = p
            dps[j, c : c + CHUNK] = dp
            delta8 = delta8 + fold(low.astype(jnp.float32) * dp, jnp.sum)
            dv = jnp.dot(low, gm, preferred_element_type=jnp.float32).astype(jnp.bfloat16)
            targets[j][1, c : c + CHUNK] = dv
    delta = jnp.sum(delta8, axis=0, keepdims=True)

    dq_t = jnp.zeros((HD, TILE), jnp.float32)
    key_gain_sum = jnp.zeros((8, HD), jnp.float32)
    for j in range(9):
        unit, _ = unit_norm(sources[j][0])
        for c in range(0, TILE, CHUNK):
            ds = (probs[j, c : c + CHUNK] * (dps[j, c : c + CHUNK] - delta) * SCALE).astype(
                jnp.bfloat16
            )
            dk = jnp.dot(ds, qn, preferred_element_type=jnp.float32).astype(jnp.bfloat16)
            targets[j][0, c : c + CHUNK] = dk
            key_gain_sum = key_gain_sum + fold(
                dk.astype(jnp.float32) * unit[c : c + CHUNK], jnp.sum
            )
            dq_t = dq_t + lax.dot_general(
                kn[j, c : c + CHUNK],
                ds,
                (((0,), (0,)), ((), ())),
                preferred_element_type=jnp.float32,
            )
    dq = dq_t.T
    d_queries[...] = norm_back(dq, q_unit, q_inverse, gain_q).astype(jnp.bfloat16)

    if head == 0:
        gains[...] = jnp.zeros_like(gains)

    gains[0:8] += fold(dq * q_unit, jnp.sum)
    gains[8:16] += key_gain_sum


def block_specs():
    row = pl.BlockSpec((TILE, HD), lambda h: (0, h))
    pair = pl.BlockSpec((2, TILE, HD), lambda h: (0, 0, h))
    whole = pl.BlockSpec((1, HD), lambda h: (0, 0))
    return row, pair, whole


def attention(frame_counts, row_counts, query_gain, key_gain, queries, grads, ins):
    heads = queries.shape[1] // HD
    row, pair, whole = block_specs()
    low = lambda *lead: jax.ShapeDtypeStruct(lead + queries.shape, jnp.bfloat16)
    return pl.pallas_call(
        attention_kernel,
        in_specs=[pl.BlockSpec(memory_space=pltpu.SMEM)] * 2
        + [pl.BlockSpec(memory_space=pltpu.VMEM)] * 13,
        out_specs=[pl.BlockSpec(memory_space=pltpu.VMEM)] * 11,
        out_shape=[low(2)] * 9 + [low(), jax.ShapeDtypeStruct((16, HD), jnp.float32)],
        scratch_shapes=[
            pltpu.VMEM((9, TILE, HD), jnp.bfloat16),
            pltpu.VMEM((9, TILE, TILE), jnp.float32),
            pltpu.VMEM((9, TILE, TILE), jnp.float32),
        ],
        compiler_params=pltpu.CompilerParams(vmem_limit_bytes=36 * 2**20),
        cost_estimate=pl.CostEstimate(
            flops=heads * 10 * TILE * TILE * 9 * HD,
            bytes_accessed=40 * TILE * queries.shape[1] * 2,
            transcendentals=heads * 9 * TILE * TILE,
        ),
    )(frame_counts, row_counts, query_gain[None], key_gain[None], queries, grads, *ins)


def finish_kernel(key_gain, keys, *rest):
    pairs, (d_keys, d_values) = rest[:-2], rest[-2:]
    for head in range(keys.shape[-1] // HD):
        part = pl.ds(head * HD, HD)
        total = pairs[0][:, :, part].astype(jnp.float32)
        for pair in pairs[1:]:
            total = total + pair[:, :, part].astype(jnp.float32)
        unit, inverse = unit_norm(keys[:, part])
        d_keys[:, part] = norm_back(total[0], unit, inverse, key_gain[...]).astype(jnp.bfloat16)
        d_values[:, part] = total[1].astype(jnp.bfloat16)


def finish(key_gain, keys, pairs):
    return pl.pallas_call(
        finish_kernel,
        in_specs=[pl.BlockSpec(memory_space=pltpu.VMEM)] * (2 + len(pairs)),
        out_specs=[pl.BlockSpec(memory_space=pltpu.VMEM)] * 2,
        out_shape=[jax.ShapeDtypeStruct(keys.shape, jnp.bfloat16)] * 2,
        compiler_params=pltpu.CompilerParams(vmem_limit_bytes=24 * 2**20),
    )(key_gain[None], keys, *pairs)


def swaps(size, first, skip=()):
    route = []
    for i in range(first, size - 1, 2):
        if i not in skip:
            route += [(i, i + 1), (i + 1, i)]
    return route


def total_over(x, axis, bits):
    size = lax.axis_size(axis)
    for bit in bits:
        x = x + lax.ppermute(x, axis, [(i, i ^ bit) for i in range(size)])
    return x


def on_device(
    queries, key_vectors, value_vectors, out_grads, query_gain, key_gain, frame_counts, row_counts
):
    time_count = lax.axis_size("tm")
    height_count = lax.axis_size("height")
    row_count = queries.shape[2]
    feature_count = queries.shape[3]
    keys = key_vectors[0, 0]
    values = value_vectors[0, 0]

    even_t, odd_t = swaps(8, 0), swaps(8, 1, (3,))
    even_h, odd_h = swaps(4, 0), swaps(4, 1)
    key_route = odd_t + [(3, 4), (4, 3)]
    value_route = odd_t + [(3, 0), (4, 7)]
    arrive = [(0, 4), (7, 3)]
    time_index = lax.axis_index("tm")
    across = (time_index == 3) | (time_index == 4)

    tv = lax.ppermute(values, "tm", value_route)
    tk = lax.ppermute(keys, "tm", key_route)
    own = jnp.stack([keys, values])
    he = lax.ppermute(own, "height", even_h)
    ho = lax.ppermute(own, "height", odd_h)
    te = lax.ppermute(own, "tm", even_t)
    vx = lax.ppermute(tv, "tm", arrive)
    he, ho, te = lax.optimization_barrier((he, ho, te))
    ce = lax.ppermute(he, "tm", even_t)
    co = lax.ppermute(ho, "tm", even_t)
    to = jnp.stack([tk, jnp.where(across, vx, tv)])
    ze = lax.ppermute(to, "height", even_h)
    zo = lax.ppermute(to, "height", odd_h)

    outs = attention(
        frame_counts,
        row_counts,
        query_gain,
        key_gain,
        queries[0, 0],
        out_grads[0, 0],
        [own, te, to, he, ho, ce, co, ze, zo],
    )
    own, te, to, he, ho, ce, co, ze, zo, d_queries, gain_parts = outs

    def add(*parts):
        return sum(x.astype(jnp.float32) for x in parts).astype(jnp.bfloat16)

    ze = lax.ppermute(ze, "height", even_h)
    zo = lax.ppermute(zo, "height", odd_h)
    ce = lax.ppermute(ce, "tm", even_t)
    co = lax.ppermute(co, "tm", even_t)
    gain_local = jnp.sum(gain_parts.reshape(2, 8, HD), axis=1)
    gain_local = total_over(total_over(gain_local, "tm", (3,)), "dp", (1, 2))
    gain_local, ze, zo = lax.optimization_barrier((gain_local, ze, zo))
    to = add(to, ze, zo)
    gain_local, _ = lax.optimization_barrier((gain_local, to))
    to = lax.ppermute(to, "tm", key_route)
    he = lax.ppermute(add(he, ce), "height", even_h)
    ho = lax.ppermute(add(ho, co), "height", odd_h)
    gain_local = total_over(total_over(gain_local, "dp", (4,)), "tm", (1,))
    gain_local, te = lax.optimization_barrier((gain_local, te))
    te = lax.ppermute(te, "tm", even_t)
    inner = [t for t in range(8) if t % 4 in (1, 2)]
    x = gain_local
    x = x + lax.ppermute(x, "tm", [(t, t ^ 4) for t in inner])
    for bit in (1, 2):
        route = [(4 * t + h, 4 * t + (h ^ bit)) for t in inner for h in range(4)]
        x = x + lax.ppermute(x, ("tm", "height"), route)
    outer = lax.ppermute(x, "tm", [(1, 0), (2, 3), (5, 4), (6, 7)])
    place = lax.rem(lax.axis_index("tm"), 4)
    gain_total = jnp.where((place == 1) | (place == 2), x, outer)
    d_keys, d_values = finish(key_gain, keys, [own, te, to, he, ho])

    head_total = lax.axis_size("dp") * (feature_count // HD)
    scaling = 1.0 / math.sqrt(time_count * height_count * row_count * head_total)
    gain_grads = gain_total * scaling
    return (d_queries[None, None], d_keys[None, None], d_values[None, None], gain_grads)


def solution(mesh):
    split = P("tm", "height", None, "dp")
    return jax.shard_map(
        on_device,
        mesh=mesh,
        in_specs=(split,) * 4 + (P(),) * 4,
        out_specs=(split,) * 3 + (P(),),
        check_vma=False,
    )
```
